32 devices in a mesh: groups: 2 (over x), tensor: 16 (over z, y, core).
Axes of the slice: x: 2, y: 2, z: 4, core: 2. Of those that a mesh axis runs over, the one named last changes fastest.
Arguments:
- input_queries: bfloat16 [4096, 3072], P(('groups', 'tensor')), parts along dimension 0, may hold values from -110 to 110
- input_keys: bfloat16 [4096, 3072], P(('groups', 'tensor')), parts along dimension 0, may hold values from -4.5 to 4.5, as said below
- input_values: bfloat16 [4096, 3072], P(('groups', 'tensor')), parts along dimension 0, may hold values from -12 to 12
- output_matrix: bfloat16 [3072, 3072], P('tensor'), may hold values from -0.109375 to 0.109375
- adapter_down_weight: bfloat16 [3072, 64], replicated, may hold values from -0.109375 to 0.109375
- adapter_up_weight: bfloat16 [64, 3072], replicated, may hold values from -0.75 to 0.75
- upstream: bfloat16 [4096, 3072], P(('groups', 'tensor')), parts along dimension 0, may hold values from -6 to 6
- window_frame_reach: int32 [24], replicated, may hold values from 0 to 1, as said below
- window_row_reach: int32 [24], replicated, may hold values from 0 to 1, as said below
Outputs:
- projected_output: bfloat16 [4096, 3072], P(('groups', 'tensor')), parts along dimension 0
- grad_query: bfloat16 [4096, 3072], P(('groups', 'tensor')), parts along dimension 0
- grad_key: bfloat16 [4096, 3072], P(('groups', 'tensor')), parts along dimension 0
- grad_value: bfloat16 [4096, 3072], P(('groups', 'tensor')), parts along dimension 0
- grad_down: float32 [6144, 64], P('groups'), parts along dimension 0
- up_weight_gradient: float32 [128, 3072], P('groups'), parts along dimension 0
The draws below stay inside these ranges and needn't reach their ends.
There are 2 independent parts, one for each index of `groups`. The reference program is written for one: setup_inputs(seed, part) draws one part's arguments, and reference() takes and returns one part's arrays. A program takes and returns all parts, laid end to end along the dimension named above; an argument that names none is the same for every part. Nothing has to cross between parts.
Inputs may be any that keep to these rules, and one draw needn't show every extreme that they name: `input_keys`: keys are standard normal draws cut at 4.5. `window_frame_reach`: some head has reach 0 and some head reach 1. `window_row_reach`: some head has reach 0 and some head reach 1.
All inputs are finite; a program needn't handle non-finite values.
Results may differ from the reference program's by a relative error of at most 0.015.
Values may be sent and summed in bfloat16 or wider, within the bound.
No kernel may reach another device: no remote copies, remote signals or barrier semaphores. Data moves between devices by JAX's collectives and lax.ppermute only.
A program may use at most 128 MiB of HBM per device.

```python
import jax
import jax.numpy as jnp
from jax import lax

MODEL_WIDTH = 3072
HEADS = 24
ADAPTER_RANK = 64
ROWS = 8
COLS = 64
CTILES = 4
BANDS = 2
RIM = 1
CRIM = 1
TCOLS = 16
TOK_DEV = 128
KEYS = 540
HEIGHT = 16
FRAMES = 2
TOKENS = 2048


def shared_keys(key):
    return jnp.clip(jax.random.normal(key, (TOKENS, MODEL_WIDTH), jnp.float32), -4.5, 4.5)


def draw_input_keys(key, part):
    return shared_keys(key).astype(jnp.bfloat16)


def draw_input_queries(key, part):
    key = jax.random.fold_in(key, 7)
    fresh = jnp.clip(jax.random.normal(key, (TOKENS, MODEL_WIDTH), jnp.float32), -4.5, 4.5)
    return fresh.astype(jnp.bfloat16)


def mixed_reach(key, largest):
    bits_key, order_key = jax.random.split(key)
    reach = jax.random.randint(bits_key, (HEADS,), 0, largest + 1).astype(jnp.int32)
    order = jax.random.permutation(order_key, HEADS)
    reach = reach.at[order[0]].set(0)
    reach = reach.at[order[1]].set(largest)
    return reach.astype(jnp.int32)


def draw_window_frame_reach(key, part):
    key = jax.random.fold_in(key, 11)
    return mixed_reach(key, 1)


def draw_window_row_reach(key, part):
    key = jax.random.fold_in(key, 13)
    return mixed_reach(key, RIM)


def steps_of(own_key, shape, cuts, low, top_value):
    level = 1.0
    for position, parts in cuts:
        heights = jax.random.uniform(jax.random.fold_in(jax.random.fold_in(own_key, 6), position), (parts,), jnp.float32, low / len(cuts), top_value / len(cuts))
        level = level * jnp.repeat(jnp.exp(heights), shape[position] // parts).reshape((-1,) + (1,) * (len(shape) - 1 - position))
    return level


def bell_draw(stream_key, shape, scale, most, pieces=(), kind=jnp.bfloat16):
    factor_of = steps_of(stream_key, shape, pieces, -0.22, 0.18) if pieces else 1.0
    array = jax.random.normal(stream_key, shape, jnp.float32) * scale * factor_of
    return jnp.minimum(jnp.maximum(array, -most), most).astype(kind)


def setup_inputs(seed: int = 0, part: int = 0) -> dict:
    keys = jax.random.split(jax.random.key(seed), 10)
    part_splits = jax.random.split(jax.random.fold_in(keys[9], part), 10)
    return {
        "input_queries": draw_input_queries(jax.random.fold_in(jax.random.fold_in(keys[9], part), 71), part),
        "input_keys": draw_input_keys(jax.random.fold_in(jax.random.fold_in(keys[9], part), 71), part),
        "input_values": bell_draw(part_splits[2], (TOKENS, MODEL_WIDTH), 3.0, 12.0, ((0, 16),)),
        "output_matrix": bell_draw(keys[3], (MODEL_WIDTH, MODEL_WIDTH), MODEL_WIDTH ** -0.5, 0.109375, ((0, 16),)),
        "adapter_down_weight": bell_draw(keys[4], (MODEL_WIDTH, ADAPTER_RANK), MODEL_WIDTH ** -0.5, 0.109375),
        "adapter_up_weight": bell_draw(keys[5], (ADAPTER_RANK, MODEL_WIDTH), ADAPTER_RANK ** -0.5, 0.75),
        "upstream": bell_draw(part_splits[6], (TOKENS, MODEL_WIDTH), 1.0, 6.0, ((0, 16),)),
        "window_frame_reach": draw_window_frame_reach(jax.random.fold_in(keys[9], 71), part),
        "window_row_reach": draw_window_row_reach(jax.random.fold_in(keys[9], 71), part),
    }


adapter_scale = 0.5


def window_table(frame_idx, band_idx, col_idx, frames, window_frame_reach, window_row_reach):
    extent = ROWS + 2 * RIM
    span = TCOLS + 2 * CRIM
    shifts = jnp.arange(3, dtype=jnp.int32) - 1
    frame_ok = (frame_idx + shifts >= 0) & (frame_idx + shifts < frames)
    key_height = band_idx * ROWS - RIM + jnp.arange(extent, dtype=jnp.int32)
    height_ok = (key_height >= 0) & (key_height < BANDS * ROWS)
    query_height = band_idx * ROWS + jnp.arange(ROWS, dtype=jnp.int32)
    height_gap = jnp.abs(key_height[None, :] - query_height[:, None])
    key_column = col_idx * TCOLS - CRIM + jnp.arange(span, dtype=jnp.int32)
    column_ok = (key_column >= 0) & (key_column < CTILES * TCOLS)
    query_column = col_idx * TCOLS + jnp.arange(TCOLS, dtype=jnp.int32)
    column_gap = jnp.abs(key_column[None, :] - query_column[:, None])
    width_fit = (column_gap <= CRIM) & column_ok[None, :]
    time_fit = (jnp.abs(shifts)[None, :] <= window_frame_reach[:, None]) & frame_ok[None, :]
    height_fit = (height_gap[None] <= window_row_reach[:, None, None]) & height_ok[None, None, :]
    allowed = time_fit[:, None, None, :, None, None] & height_fit[:, :, None, None, :, None] & width_fit[None, None, :, None, None, :]
    return allowed.reshape(window_frame_reach.shape[0], ROWS * TCOLS, 3 * extent * span)


def split_heads(block, heads):
    return block.astype(jnp.float32).reshape(block.shape[0], heads, -1)


def tile_scores(query_heads, key_heads, allowed):
    scale = query_heads.shape[2] ** -0.5
    scores = jnp.einsum('qhd,khd->hqk', query_heads, key_heads, precision=lax.Precision.HIGHEST) * scale
    return jnp.where(allowed, scores, -1e30)


def attend_tile(query_tile, key_block, value_block, allowed):
    heads = allowed.shape[0]
    query_heads = split_heads(query_tile, heads)
    key_heads = split_heads(key_block, heads)
    value_heads = split_heads(value_block, heads)
    scores = tile_scores(query_heads, key_heads, allowed)
    row_max = jnp.max(scores, axis=2, keepdims=True)
    weights = jnp.exp(scores - row_max)
    totals = jnp.sum(weights, axis=2)
    weights_low = weights.astype(jnp.bfloat16).astype(jnp.float32)
    mixed = jnp.einsum('hqk,khd->qhd', weights_low, value_heads, precision=lax.Precision.HIGHEST)
    attention_result = (mixed / totals.T[:, :, None]).astype(jnp.bfloat16).reshape(query_tile.shape)
    return attention_result, row_max[:, :, 0] + jnp.log(totals)


def attend_back(query_tile, key_block, value_block, allowed, attention_result, attention_gradient, log_total):
    heads = allowed.shape[0]
    query_heads = split_heads(query_tile, heads)
    key_heads = split_heads(key_block, heads)
    value_heads = split_heads(value_block, heads)
    grad_heads = split_heads(attention_gradient, heads)
    attended_heads = split_heads(attention_result, heads)
    scale = query_heads.shape[2] ** -0.5
    scores = tile_scores(query_heads, key_heads, allowed)
    probs = jnp.exp(scores - log_total[:, :, None])
    probs_low = probs.astype(jnp.bfloat16).astype(jnp.float32)
    value_terms = jnp.einsum('hqk,qhd->khd', probs_low, grad_heads, precision=lax.Precision.HIGHEST).astype(jnp.bfloat16)
    grad_probs = jnp.einsum('qhd,khd->hqk', grad_heads, value_heads, precision=lax.Precision.HIGHEST)
    inner = jnp.sum(grad_heads * attended_heads, axis=2).T
    grad_scores = (probs * (grad_probs - inner[:, :, None])).astype(jnp.bfloat16).astype(jnp.float32)
    grad_query = (jnp.einsum('hqk,khd->qhd', grad_scores, key_heads, precision=lax.Precision.HIGHEST) * scale).astype(jnp.bfloat16)
    key_terms = (jnp.einsum('hqk,qhd->khd', grad_scores, query_heads, precision=lax.Precision.HIGHEST) * scale).astype(jnp.bfloat16)
    return grad_query.reshape(query_tile.shape), key_terms.reshape(key_block.shape), value_terms.reshape(key_block.shape)


def to_grid(token_rows):
    width = token_rows.shape[1]
    grid = token_rows.reshape(BANDS, CTILES, FRAMES, ROWS, TCOLS, width)
    return grid.transpose(2, 0, 3, 1, 4, 5).reshape(FRAMES, BANDS * ROWS, CTILES * TCOLS, width)


def from_grid(grid):
    width = grid.shape[3]
    tiles = grid.reshape(FRAMES, BANDS, ROWS, CTILES, TCOLS, width).transpose(1, 3, 0, 2, 4, 5)
    return tiles.reshape(FRAMES * BANDS * CTILES * ROWS * TCOLS, width)


def reference(input_queries, input_keys, input_values, output_matrix, adapter_down_weight, adapter_up_weight, upstream, window_frame_reach, window_row_reach):
    extent = ROWS + 2 * RIM
    span = TCOLS + 2 * CRIM
    tiles = FRAMES * BANDS * CTILES
    width = input_keys.shape[1]
    zero = jnp.zeros((), jnp.int32)
    padding = ((1, 1), (RIM, RIM), (CRIM, CRIM), (0, 0))
    key_pad = jnp.pad(to_grid(input_keys), padding)
    value_pad = jnp.pad(to_grid(input_values), padding)
    query_tiles = input_queries.reshape(tiles, TOK_DEV, width)
    shape_three = (3, extent, span, width)

    def neighbourhood(number):
        frame_idx = (number % FRAMES).astype(jnp.int32)
        band_idx = (number // (CTILES * FRAMES)).astype(jnp.int32)
        col_idx = ((number // FRAMES) % CTILES).astype(jnp.int32)
        corner = (frame_idx, band_idx * ROWS, col_idx * TCOLS, zero)
        key_block = lax.dynamic_slice(key_pad, corner, shape_three).reshape(KEYS, width)
        value_block = lax.dynamic_slice(value_pad, corner, shape_three).reshape(KEYS, width)
        allowed = window_table(frame_idx, band_idx, col_idx, FRAMES, window_frame_reach, window_row_reach)
        return corner, key_block, value_block, allowed

    def forward_tile(number):
        corner, key_block, value_block, allowed = neighbourhood(number)
        return attend_tile(query_tiles[number], key_block, value_block, allowed)

    numbers = jnp.arange(tiles, dtype=jnp.int32)
    attended_tiles, log_totals = lax.map(forward_tile, numbers)
    attention_result = attended_tiles.reshape(TOKENS, width)
    reduced_rows = jnp.dot(attention_result, adapter_down_weight, preferred_element_type=jnp.float32).astype(jnp.bfloat16)
    frozen_path_output = jnp.dot(attention_result, output_matrix, preferred_element_type=jnp.float32)
    projected_output = (frozen_path_output + adapter_scale * jnp.dot(reduced_rows, adapter_up_weight, preferred_element_type=jnp.float32)).astype(jnp.bfloat16)
    up_weight_gradient = adapter_scale * jnp.dot(reduced_rows.T, upstream, preferred_element_type=jnp.float32)
    reduced_gradient = (adapter_scale * jnp.dot(upstream, adapter_up_weight.T, preferred_element_type=jnp.float32)).astype(jnp.bfloat16)
    grad_down = jnp.dot(attention_result.T, reduced_gradient, preferred_element_type=jnp.float32)
    attention_gradient = (jnp.dot(upstream, output_matrix.T, preferred_element_type=jnp.float32) + jnp.dot(reduced_gradient, adapter_down_weight.T, preferred_element_type=jnp.float32)).astype(jnp.bfloat16)
    grad_tiles = attention_gradient.reshape(tiles, TOK_DEV, width)

    def back_tile(carry, number):
        key_acc, value_acc = carry
        corner, key_block, value_block, allowed = neighbourhood(number)
        grad_query, key_terms, value_terms = attend_back(query_tiles[number], key_block, value_block, allowed, attended_tiles[number], grad_tiles[number], log_totals[number])
        key_acc = lax.dynamic_update_slice(key_acc, lax.dynamic_slice(key_acc, corner, shape_three) + key_terms.astype(jnp.float32).reshape(shape_three), corner)
        value_acc = lax.dynamic_update_slice(value_acc, lax.dynamic_slice(value_acc, corner, shape_three) + value_terms.astype(jnp.float32).reshape(shape_three), corner)
        return (key_acc, value_acc), grad_query

    empty = jnp.zeros(key_pad.shape, jnp.float32)
    (key_acc, value_acc), grad_queries = lax.scan(back_tile, (empty, empty), numbers)
    grad_key = from_grid(key_acc[1:-1, RIM:RIM + HEIGHT, CRIM:CRIM + COLS]).astype(jnp.bfloat16)
    grad_value = from_grid(value_acc[1:-1, RIM:RIM + HEIGHT, CRIM:CRIM + COLS]).astype(jnp.bfloat16)
    grad_query = grad_queries.reshape(TOKENS, width)
    return projected_output, grad_query, grad_key, grad_value, grad_down, up_weight_gradient
```

```python
import functools

import jax
import jax.numpy as jnp
from jax import lax
from jax.experimental import pallas as pl
from jax.experimental.pallas import tpu as pltpu
from jax.sharding import PartitionSpec as P

ROWS = 8
CTILES = 4
BANDS = 2
TCOLS = 16
TILE = ROWS * TCOLS
RIM = 48
SLOT = TILE + RIM
HEAD = 128
STEP = 4

SCALE = HEAD**-0.5
ADAPTER = 0.5
F32 = jnp.float32
BF16 = jnp.bfloat16


def nn(a, b):
    return jnp.dot(a, b, preferred_element_type=F32)


def nt(a, b):
    return lax.dot_general(a, b, (((1,), (1,)), ((), ())), preferred_element_type=F32)


def tn(a, b):
    return lax.dot_general(a, b, (((0,), (0,)), ((), ())), preferred_element_type=F32)


def slot_keys(slots, cols):
    keys, values = [], []
    for core_keys, core_values, rim in slots:
        keys += [core_keys[:, cols], rim[:RIM, cols]]
        values += [core_values[:, cols], rim[RIM:, cols]]
    return jnp.concatenate(keys, axis=0), jnp.concatenate(values, axis=0)


def forward_kernel(n_slots, combo, query, *refs):
    slots = [refs[3 * i : 3 * i + 3] for i in range(n_slots)]
    bias, down, grad_low, upstream, att_ref, log_ref, grads_ref, low_ref, low_acc = refs[
        3 * n_slots :
    ]
    step = pl.program_id(0)
    rank = down.shape[0]

    @pl.when(step == 0)
    def _():
        low_acc[...] = jnp.zeros_like(low_acc)

    for i in range(STEP):
        cols = slice(i * HEAD, (i + 1) * HEAD)
        keys, values = slot_keys(slots, cols)
        scores = nt(keys, query[:, cols]) * SCALE + bias[combo[step * STEP + i]]
        top = jnp.max(scores, axis=0, keepdims=True)
        weights = jnp.exp(scores - top)
        totals = jnp.sum(weights, axis=0, keepdims=True)
        att = (tn(values, weights.astype(BF16)) / totals).astype(BF16)
        att_ref[cols, :] = att
        log_ref[0, i : i + 1, :] = top + jnp.log(totals)
        low_acc[...] += nn(down[:, cols], att)
        grads_ref[:rank, pl.ds(pl.multiple_of((step * STEP + i) * HEAD, HEAD), HEAD)] = nt(
            grad_low[...], att
        )

    @pl.when(step == pl.num_programs(0) - 1)
    def _():
        low = low_acc[...].astype(BF16)
        low_ref[...] = low
        grads_ref[rank:, :] = ADAPTER * nn(low, upstream[...])


def backward_kernel(n_slots, combo, query, *refs):
    slots = [refs[3 * i : 3 * i + 3] for i in range(n_slots)]
    bias, att, grad, log_total, grad_query = refs[3 * n_slots : 3 * n_slots + 5]
    terms = refs[3 * n_slots + 5 :]
    step = pl.program_id(0)
    for i in range(STEP):
        cols = slice(i * HEAD, (i + 1) * HEAD)
        keys, values = slot_keys(slots, cols)
        here = query[:, cols]
        scores = nt(keys, here) * SCALE + bias[combo[step * STEP + i]]
        probs = jnp.exp(scores - log_total[0, i : i + 1, :])
        grad_att = grad[cols, :]
        inner = jnp.sum(
            grad_att.astype(F32) * att[cols, :].astype(F32), axis=0, keepdims=True
        )
        value_terms = nt(probs.astype(BF16), grad_att).astype(BF16)
        grad_scores = (probs * (nn(values, grad_att) - inner)).astype(BF16)
        key_terms = (nn(grad_scores, here) * SCALE).astype(BF16)
        grad_query[:, cols] = (tn(grad_scores, keys) * SCALE).astype(BF16)
        for s in range(n_slots):
            core, rim = terms[2 * s : 2 * s + 2]
            at = s * SLOT
            core[:TILE, cols] = key_terms[at : at + TILE]
            core[TILE:, cols] = value_terms[at : at + TILE]
            rim[:RIM, cols] = key_terms[at + TILE : at + SLOT]
            rim[RIM:, cols] = value_terms[at + TILE : at + SLOT]


def column_block(rows):
    return pl.BlockSpec((rows, STEP * HEAD), lambda step, *_: (0, step))


def row_block():
    return pl.BlockSpec((STEP * HEAD, TILE), lambda step, *_: (step, 0))


def whole(shape):
    return pl.BlockSpec(shape, lambda *_: (0,) * len(shape))


def head_call(kernel, steps, in_specs, out_specs, out_shape, scratch, flops):
    return pl.pallas_call(
        kernel,
        grid_spec=pltpu.PrefetchScalarGridSpec(
            num_scalar_prefetch=1,
            grid=(steps,),
            in_specs=in_specs,
            out_specs=out_specs,
            scratch_shapes=scratch,
        ),
        out_shape=out_shape,
        compiler_params=pltpu.CompilerParams(
            dimension_semantics=("arbitrary",), vmem_limit_bytes=40 * 1024 * 1024
        ),
        cost_estimate=pl.CostEstimate(
            flops=flops, bytes_accessed=6_000_000, transcendentals=0
        ),
    )


def slot_specs(n_slots):
    return [column_block(TILE), column_block(TILE), column_block(2 * RIM)] * n_slots


def attend(combo, query, slots, bias, down, grad_low, upstream):
    tokens, width = query.shape
    heads = width // HEAD
    rank = down.shape[0]
    n_slots = len(slots)
    keys = n_slots * SLOT
    return head_call(
        functools.partial(forward_kernel, n_slots),
        heads // STEP,
        [column_block(tokens)]
        + slot_specs(n_slots)
        + [
            whole(bias.shape),
            column_block(rank),
            whole(grad_low.shape),
            whole(upstream.shape),
        ],
        [
            row_block(),
            pl.BlockSpec((1, STEP, tokens), lambda step, *_: (step, 0, 0)),
            whole((2 * rank, width)),
            whole((rank, tokens)),
        ],
        [
            jax.ShapeDtypeStruct((width, tokens), BF16),
            jax.ShapeDtypeStruct((heads // STEP, STEP, tokens), F32),
            jax.ShapeDtypeStruct((2 * rank, width), F32),
            jax.ShapeDtypeStruct((rank, tokens), BF16),
        ],
        [pltpu.VMEM((rank, tokens), F32)],
        4 * keys * tokens * width,
    )(combo, query, *[part for slot in slots for part in slot], bias, down, grad_low, upstream)


def attend_back(combo, query, slots, bias, att, grad, log_total):
    tokens, width = query.shape
    heads = width // HEAD
    n_slots = len(slots)
    keys = n_slots * SLOT
    out = head_call(
        functools.partial(backward_kernel, n_slots),
        heads // STEP,
        [column_block(tokens)]
        + slot_specs(n_slots)
        + [
            whole(bias.shape),
            row_block(),
            row_block(),
            pl.BlockSpec((1, STEP, tokens), lambda step, *_: (step, 0, 0)),
        ],
        [column_block(tokens)] + [column_block(2 * TILE), column_block(2 * RIM)] * n_slots,
        [jax.ShapeDtypeStruct((tokens, width), BF16)]
        + [
            jax.ShapeDtypeStruct((2 * TILE, width), BF16),
            jax.ShapeDtypeStruct((2 * RIM, width), BF16),
        ]
        * n_slots,
        [],
        10 * keys * tokens * width,
    )(combo, query, *[part for slot in slots for part in slot], bias, att, grad, log_total)
    return out[0], [out[1 + 2 * s : 3 + 2 * s] for s in range(n_slots)]


def window_bias(shifts, frame_idx, band_idx, col_idx, frames):
    at = jnp.arange(SLOT, dtype=jnp.int32)
    rim = at - TILE
    outer = jnp.where(band_idx == 0, ROWS, -1)
    row = jnp.where(at < TILE, at // TCOLS, jnp.where(rim < 16, rim % ROWS, outer))
    col = jnp.where(
        at < TILE,
        at % TCOLS,
        jnp.where(
            rim < 8,
            -1,
            jnp.where(
                rim < 16, TCOLS, jnp.where(rim < 32, rim - 16, jnp.where(rim == 32, -1, TCOLS))
            ),
        ),
    )
    height = band_idx * ROWS + row
    across = col_idx * TCOLS + col
    there = (height >= 0) & (height < BANDS * ROWS) & (across >= 0) & (across < CTILES * TCOLS)
    there &= rim < 34
    query = jnp.arange(TILE, dtype=jnp.int32)
    row_gap = jnp.abs(row[:, None] - (query // TCOLS)[None, :])
    col_gap = jnp.abs(col[:, None] - (query % TCOLS)[None, :])
    near = there[:, None] & (col_gap <= 1)
    reach = jnp.arange(2, dtype=jnp.int32)
    space = near[None] & (row_gap[None] <= reach[:, None, None])
    shift = jnp.array(shifts, dtype=jnp.int32)
    time = (jnp.abs(shift)[None, :] <= reach[:, None]) & (
        (frame_idx + shift >= 0) & (frame_idx + shift < frames) | (frames == 2)
    )
    allowed = time[:, None, :, None, None] & space[None, :, None, :, :]
    return jnp.where(allowed, 0.0, -1e30).astype(F32).reshape(4, len(shifts) * SLOT, TILE)


def permute(block, route):
    return lax.ppermute(block, "tensor", route)


def on_device(
    input_queries,
    input_keys,
    input_values,
    output_matrix,
    adapter_down_weight,
    adapter_up_weight,
    upstream,
    window_frame_reach,
    window_row_reach,
):
    devices = lax.axis_size("tensor")
    frames = devices // (BANDS * CTILES)
    position = lax.axis_index("tensor")
    frame_idx = position % frames
    col_idx = position // frames % CTILES
    band_idx = position // (frames * CTILES)
    everyone = range(devices)
    to_right = [(i, i + frames) for i in everyone if i // frames % CTILES < CTILES - 1]
    to_left = [(j, i) for i, j in to_right]
    to_band = [(i, (i + devices // BANDS) % devices) for i in everyone]
    if frames == 1:
        shifts, to_frame = [0], []
    elif frames == 2:
        shifts, to_frame = [0, 1], [[(i, i ^ 1) for i in everyone]]
    else:
        later = [(i, i + 1) for i in everyone if i % frames < frames - 1]
        shifts, to_frame = [0, -1, 1], [later, [(j, i) for i, j in later]]
    edge_row = jnp.where(band_idx == 0, ROWS - 1, 0)
    combo = 2 * window_frame_reach + window_row_reach

    cell = jnp.arange(TILE, dtype=jnp.int32)
    mark = jnp.arange(32, dtype=jnp.int32)
    source = jnp.where(
        mark < 8,
        mark * TCOLS,
        jnp.where(mark < 16, (mark - 8) * TCOLS + TCOLS - 1, edge_row * TCOLS + mark - 16),
    )
    pick = (source[:, None] == cell[None, :]).astype(BF16)
    edge_keys = nn(pick, input_keys).astype(BF16)
    edge_values = nn(pick, input_values).astype(BF16)
    right = permute(jnp.concatenate([edge_keys[:8], edge_values[:8]]), to_left)
    left = permute(jnp.concatenate([edge_keys[8:16], edge_values[8:16]]), to_right)
    core_slots = [
        (permute(input_keys, route), permute(input_values, route)) for route in to_frame
    ]

    def corner(block, at):
        return lax.dynamic_slice_in_dim(block, at + edge_row, 1)

    outer = permute(
        jnp.concatenate(
            [
                edge_keys[16:],
                edge_values[16:],
                corner(left, 0),
                corner(right, 0),
                corner(left, 8),
                corner(right, 8),
            ]
        ),
        to_band,
    )
    blank = jnp.zeros((14, input_keys.shape[1]), BF16)
    rim = jnp.concatenate(
        [
            left[:8], right[:8], outer[:16], outer[32:34], blank,
            left[8:], right[8:], outer[16:32], outer[34:], blank,
        ]
    )
    slots = [(input_keys, input_values, rim)] + [
        (*core, permute(rim, route)) for core, route in zip(core_slots, to_frame)
    ]
    bias = window_bias(shifts, frame_idx, band_idx, col_idx, frames)

    whole_weight = lax.all_gather(output_matrix, "tensor", axis=0, tiled=True)
    down = adapter_down_weight.T
    grad_low = (ADAPTER * nt(adapter_up_weight, upstream)).astype(BF16)
    att, log_total, grads, low = attend(
        combo, input_queries, slots, bias, down, grad_low, upstream
    )

    def rounded(block):
        return block.astype(BF16).astype(F32)

    rank = down.shape[0]
    second = position % 2
    mine = lax.dynamic_slice_in_dim(grads, second * rank, rank)
    theirs = lax.dynamic_slice_in_dim(grads, (1 - second) * rank, rank).astype(BF16)
    part = mine + permute(theirs, [(i, i ^ 1) for i in everyone]).astype(F32)
    bit = 2
    while bit < devices:
        part = part.astype(BF16)
        part = part.astype(F32) + permute(part, [(i, i ^ bit) for i in everyone]).astype(F32)
        bit *= 2
    part = part.astype(BF16)
    other = permute(part, [(i, i ^ 1) for i in everyone])
    grad_down = jnp.where(second == 0, part, other).astype(F32).T
    grad_up = jnp.where(second == 0, other, part).astype(F32)

    grad_att = (nt(whole_weight, upstream) + tn(down, grad_low)).astype(BF16)
    grad_query, terms = attend_back(
        combo, input_queries, slots, bias, att, grad_att, log_total
    )
    projected = (
        tn(att, whole_weight) + ADAPTER * tn(low, adapter_up_weight)
    ).astype(BF16)

    core, rim_terms = terms[0]
    rim_terms = rim_terms.astype(F32)
    back = [[(j, i) for i, j in route] for route in to_frame]
    for (_, sent), route in zip(terms[1:], back):
        rim_terms += permute(sent, route).astype(F32)
    core_terms = [core] + [permute(sent, route) for (sent, _), route in zip(terms[1:], back)]
    keys_out, values_out = rim_terms[:RIM], rim_terms[RIM:]
    outer = permute(
        jnp.concatenate(
            [keys_out[16:32], values_out[16:32], keys_out[32:34], values_out[32:34]]
        ).astype(BF16),
        to_band,
    )
    at_edge = (jnp.arange(ROWS)[:, None] == edge_row).astype(F32)
    outer_corners = outer[32:].astype(F32)

    def side(number):
        at = 8 * number
        return jnp.concatenate(
            [
                keys_out[at : at + 8] + at_edge * outer_corners[number],
                values_out[at : at + 8] + at_edge * outer_corners[2 + number],
            ]
        ).astype(BF16)

    from_right = permute(side(0), to_left)
    from_left = permute(side(1), to_right)
    gathered = [
        jnp.concatenate([from_left[at : at + 8], from_right[at : at + 8], outer[row : row + 16]])
        for at, row in ((0, 0), (8, 16))
    ]
    grad_key, grad_value = (
        (
            sum(block[rows].astype(F32) for block in core_terms) + tn(pick, got)
        ).astype(BF16)
        for rows, got in ((slice(0, TILE), gathered[0]), (slice(TILE, None), gathered[1]))
    )
    return (projected, grad_query, grad_key, grad_value, grad_down, grad_up)


def solution(mesh):
    tokens = P(("groups", "tensor"), None)
    return jax.shard_map(
        on_device,
        mesh=mesh,
        in_specs=(tokens, tokens, tokens, P("tensor", None), P(), P(), tokens, P(), P()),
        out_specs=(tokens, tokens, tokens, tokens, P("groups", None), P("groups", None)),
        check_vma=False,
    )
```

```python
import functools

import jax
import jax.numpy as jnp
from jax import lax
from jax.experimental import pallas as pl
from jax.experimental.pallas import tpu as pltpu
from jax.sharding import PartitionSpec as P

ROWS = 8
CTILES = 4
BANDS = 2
TCOLS = 16
TILE = ROWS * TCOLS
RIM = 48
SLOT = TILE + RIM
HEAD = 128
STEP = 4

SCALE = HEAD**-0.5
ADAPTER = 0.5
F32 = jnp.float32
BF16 = jnp.bfloat16


def nn(a, b):
    return jnp.dot(a, b, preferred_element_type=F32)


def nt(a, b):
    return lax.dot_general(a, b, (((1,), (1,)), ((), ())), preferred_element_type=F32)


def tn(a, b):
    return lax.dot_general(a, b, (((0,), (0,)), ((), ())), preferred_element_type=F32)


def slot_keys(slots, cols):
    keys, values = [], []
    for core_keys, core_values, rim in slots:
        keys += [core_keys[:, cols], rim[:RIM, cols]]
        values += [core_values[:, cols], rim[RIM:, cols]]
    return jnp.concatenate(keys, axis=0), jnp.concatenate(values, axis=0)


def forward_kernel(n_slots, combo, query, *refs):
    slots = [refs[3 * i : 3 * i + 3] for i in range(n_slots)]
    bias, down, grad_low, upstream, att_ref, log_ref, grads_ref, low_ref, low_acc = refs[
        3 * n_slots :
    ]
    step = pl.program_id(0)
    last = combo.shape[0] - 1

    @pl.when(step == 0)
    def _():
        low_acc[...] = jnp.zeros_like(low_acc)

    for i in range(STEP):
        cols = slice(i * HEAD, (i + 1) * HEAD)
        keys, values = slot_keys(slots, cols)
        scores = nt(keys, query[:, cols]) * SCALE + bias[combo[step * STEP + i]]
        top = jnp.max(scores, axis=0, keepdims=True)
        weights = jnp.exp(scores - top)
        totals = jnp.sum(weights, axis=0, keepdims=True)
        att = (tn(values, weights.astype(BF16)) / totals).astype(BF16)
        att_ref[cols, :] = att
        log_ref[0, i : i + 1, :] = top + jnp.log(totals)
        low_acc[...] += nn(down[:, cols], att)
        at = pl.ds(pl.multiple_of((step * STEP + i) * HEAD, HEAD), HEAD)
        grads_ref[combo[last], :, at] = nt(grad_low[...], att).astype(BF16)

    @pl.when(step == pl.num_programs(0) - 1)
    def _():
        low = low_acc[...].astype(BF16)
        low_ref[...] = low
        grads_ref[1 - combo[last]] = (ADAPTER * nn(low, upstream[...])).astype(BF16)


def backward_kernel(n_slots, combo, query, *refs):
    slots = [refs[3 * i : 3 * i + 3] for i in range(n_slots)]
    bias, att, grad, extra, log_total, grad_query = refs[3 * n_slots : 3 * n_slots + 6]
    terms = refs[3 * n_slots + 6 :]
    step = pl.program_id(0)
    for i in range(STEP):
        cols = slice(i * HEAD, (i + 1) * HEAD)
        keys, values = slot_keys(slots, cols)
        here = query[:, cols]
        scores = nt(keys, here) * SCALE + bias[combo[step * STEP + i]]
        probs = jnp.exp(scores - log_total[0, i : i + 1, :])
        grad_att = (grad[cols, :].astype(F32) + extra[cols, :]).astype(BF16)
        inner = jnp.sum(
            grad_att.astype(F32) * att[cols, :].astype(F32), axis=0, keepdims=True
        )
        value_terms = nt(probs.astype(BF16), grad_att).astype(BF16)
        grad_scores = (probs * (nn(values, grad_att) - inner)).astype(BF16)
        key_terms = (nn(grad_scores, here) * SCALE).astype(BF16)
        grad_query[:, cols] = (tn(grad_scores, keys) * SCALE).astype(BF16)
        for s in range(n_slots):
            core, rim = terms[2 * s : 2 * s + 2]
            at = s * SLOT
            core[:TILE, cols] = key_terms[at : at + TILE]
            core[TILE:, cols] = value_terms[at : at + TILE]
            rim[:RIM, cols] = key_terms[at + TILE : at + SLOT]
            rim[RIM:, cols] = value_terms[at + TILE : at + SLOT]


def column_block(rows):
    return pl.BlockSpec((rows, STEP * HEAD), lambda step, *_: (0, step))


def row_block():
    return pl.BlockSpec((STEP * HEAD, TILE), lambda step, *_: (step, 0))


def whole(shape):
    return pl.BlockSpec(shape, lambda *_: (0,) * len(shape))


def head_call(kernel, steps, in_specs, out_specs, out_shape, scratch):
    call = pl.pallas_call(
        kernel,
        grid_spec=pltpu.PrefetchScalarGridSpec(
            num_scalar_prefetch=1,
            grid=(steps,),
            in_specs=in_specs,
            out_specs=out_specs,
            scratch_shapes=scratch,
        ),
        out_shape=out_shape,
        compiler_params=pltpu.CompilerParams(
            dimension_semantics=("arbitrary",), vmem_limit_bytes=14 * 1024 * 1024
        ),
        cost_estimate=pl.CostEstimate(flops=1000, bytes_accessed=1000, transcendentals=0),
    )

    def from_hbm(scalars, *arrays):
        return call(scalars, *in_hbm(arrays[:3]), *arrays[3:])

    return from_hbm


def in_hbm(arrays):
    return [pltpu.with_memory_space_constraint(array, pltpu.HBM) for array in arrays]


def slot_specs(n_slots):
    return [column_block(TILE), column_block(TILE), column_block(2 * RIM)] * n_slots


def attend(combo, query, slots, bias, down, grad_low, upstream):
    tokens, width = query.shape
    heads = width // HEAD
    rank = down.shape[0]
    n_slots = len(slots)
    return head_call(
        functools.partial(forward_kernel, n_slots),
        heads // STEP,
        [column_block(tokens)]
        + slot_specs(n_slots)
        + [
            whole(bias.shape),
            column_block(rank),
            whole(grad_low.shape),
            whole(upstream.shape),
        ],
        [
            row_block(),
            pl.BlockSpec((1, STEP, tokens), lambda step, *_: (step, 0, 0)),
            whole((2, rank, width)),
            whole((rank, tokens)),
        ],
        [
            jax.ShapeDtypeStruct((width, tokens), BF16),
            jax.ShapeDtypeStruct((heads // STEP, STEP, tokens), F32),
            jax.ShapeDtypeStruct((2, rank, width), BF16),
            jax.ShapeDtypeStruct((rank, tokens), BF16),
        ],
        [pltpu.VMEM((rank, tokens), F32)],
    )(combo, query, *[part for slot in slots for part in slot], bias, down, grad_low, upstream)


def attend_back(combo, query, slots, bias, att, grad, extra, log_total):
    tokens, width = query.shape
    heads = width // HEAD
    n_slots = len(slots)
    out = head_call(
        functools.partial(backward_kernel, n_slots),
        heads // STEP,
        [column_block(tokens)]
        + slot_specs(n_slots)
        + [
            whole(bias.shape),
            row_block(),
            row_block(),
            row_block(),
            pl.BlockSpec((1, STEP, tokens), lambda step, *_: (step, 0, 0)),
        ],
        [column_block(tokens)] + [column_block(2 * TILE), column_block(2 * RIM)] * n_slots,
        [jax.ShapeDtypeStruct((tokens, width), BF16)]
        + [
            jax.ShapeDtypeStruct((2 * TILE, width), BF16),
            jax.ShapeDtypeStruct((2 * RIM, width), BF16),
        ]
        * n_slots,
        [],
    )(
        combo, query, *[part for slot in slots for part in slot], bias, *in_hbm([att]), grad, extra,
        log_total,
    )
    return out[0], [out[1 + 2 * s : 3 + 2 * s] for s in range(n_slots)]


PLACES = [(x, y) for y in range(2) for x in range(2)]
MEMBERS = [(x, y, c) for x, y in PLACES for c in range(2)]


def block_of(member, turn):
    x, y, c = member
    return turn * 8 + y * 4 + c * 2 + x


def plain_call(kernel, grid, in_specs, out_specs, out_shape, scratch):
    return pl.pallas_call(
        kernel,
        grid=grid,
        in_specs=in_specs,
        out_specs=out_specs,
        out_shape=out_shape,
        scratch_shapes=scratch,
        compiler_params=pltpu.CompilerParams(
            dimension_semantics=("arbitrary",) * len(grid), vmem_limit_bytes=14 * 1024 * 1024
        ),
        cost_estimate=pl.CostEstimate(flops=1000, bytes_accessed=1000, transcendentals=0),
    )


def spread_kernel(turns, me, rows_ref, *outs):
    size = rows_ref.shape[0] // (8 * turns)
    for number, member in enumerate(MEMBERS):
        for turn in range(turns):
            at = pl.multiple_of((block_of(member, turn) ^ me[0]) * size, size)
            outs[number % 2][number // 2, turn * size : (turn + 1) * size, :] = rows_ref[
                pl.ds(at, size), :
            ]


def collect_kernel(turns, me, *refs):
    out = refs[-1]
    size = out.shape[0] // (8 * turns)
    for number, member in enumerate(MEMBERS):
        part = refs[number // 2].at[number % 2]
        for turn in range(turns):
            at = pl.multiple_of((block_of(member, turn) ^ me[0]) * size, size)
            out[pl.ds(at, size), :] = part[turn * size : (turn + 1) * size, :]


SCALARS = pl.BlockSpec(memory_space=pltpu.SMEM)


def spread(rows, me, turns):
    total, tokens = rows.shape
    size = total // (8 * turns)
    part = (4, turns * size, tokens)
    if size % 16:
        blocks = rows.reshape(8 * turns, size, tokens)
        order = [[block_of((x, y, c), t) for x, y in PLACES for t in range(turns)] for c in range(2)]
        return [jnp.take(blocks, me ^ jnp.array(o), axis=0).reshape(part) for o in order]
    return plain_call(
        functools.partial(spread_kernel, turns),
        (1,),
        [SCALARS, whole(rows.shape)],
        [whole(part)] * 2,
        [jax.ShapeDtypeStruct(part, rows.dtype)] * 2,
        [],
    )(me[None], *in_hbm([rows]))


def collect(parts, me, turns):
    _, rows, tokens = parts[0].shape
    size = rows // turns
    total = 8 * rows
    if size % 16:
        every = [parts[number // 2][number % 2] for number in range(8)]
        blocks = jnp.concatenate(every).reshape(8 * turns, size, tokens)
        slot = {block_of(m, t): i * turns + t for i, m in enumerate(MEMBERS) for t in range(turns)}
        order = jnp.array([slot[b] for b in range(8 * turns)])
        return jnp.take(blocks, order[me ^ jnp.arange(8 * turns)], axis=0).reshape(total, tokens)
    return plain_call(
        functools.partial(collect_kernel, turns),
        (1,),
        [SCALARS] + [whole(part.shape) for part in parts],
        whole((total, tokens)),
        jax.ShapeDtypeStruct((total, tokens), parts[0].dtype),
        [],
    )(me[None], *parts)


def edge_kernel(where, keys, values, to_left, to_right, edge):
    mark = lax.broadcasted_iota(jnp.int32, (32, TILE), 0)
    cell = lax.broadcasted_iota(jnp.int32, (32, TILE), 1)
    side = jnp.where(mark < 8, mark * TCOLS, (mark - 8) * TCOLS + TCOLS - 1)
    source = jnp.where(mark < 16, side, where[0] * TCOLS + mark - 16)
    pick = (source == cell).astype(F32).astype(BF16)
    key_edges = nn(pick, keys[...])
    value_edges = nn(pick, values[...])
    to_left[...] = jnp.concatenate([key_edges[:8], value_edges[:8]]).astype(BF16)
    to_right[...] = jnp.concatenate([key_edges[8:16], value_edges[8:16]]).astype(BF16)
    edge[...] = jnp.concatenate([key_edges[16:], value_edges[16:]]).astype(BF16)


def outer_kernel(where, left, right, edge, outer):
    sides = [left[...].astype(F32), right[...].astype(F32)]
    last = where[0] == ROWS - 1
    corners = [
        jnp.where(last, side[at + ROWS - 1 : at + ROWS], side[at : at + 1])
        for at in (0, 8)
        for side in sides
    ]
    blank = jnp.zeros((4, edge.shape[1]), F32)
    outer[...] = jnp.concatenate([edge[...].astype(F32), *corners, blank]).astype(BF16)


def rim_kernel(left, right, outer, rim):
    sides = [left[...].astype(F32), right[...].astype(F32)]
    far = outer[...].astype(F32)
    blank = jnp.zeros((14, far.shape[1]), F32)
    rim[...] = jnp.concatenate(
        [
            sides[0][:8], sides[1][:8], far[:16], far[32:34], blank,
            sides[0][8:], sides[1][8:], far[16:32], far[34:36], blank,
        ]
    ).astype(BF16)


def column_call(kernel, scalars, blocks, out_rows):
    width = blocks[0].shape[1]
    step = width // 4
    out = plain_call(
        kernel,
        (4,),
        [SCALARS] * len(scalars)
        + [pl.BlockSpec((block.shape[0], step), lambda j: (0, j)) for block in blocks],
        [pl.BlockSpec((rows, step), lambda j: (0, j)) for rows in out_rows],
        [jax.ShapeDtypeStruct((rows, width), BF16) for rows in out_rows],
        [],
    )(*scalars, *blocks)
    return out if len(out_rows) > 1 else out[0]


def pack_kernel(here, there, *outs):
    for place, out in enumerate(outs):
        out[0] = here[place]
        out[1] = there[place]


def pack(here, there):
    _, rows, tokens = here.shape
    return plain_call(
        pack_kernel,
        (1,),
        [whole(here.shape)] * 2,
        [whole((2, rows, tokens))] * 4,
        [jax.ShapeDtypeStruct((2, rows, tokens), BF16)] * 4,
        [],
    )(here, there)


def weight_block(refs):
    return jnp.concatenate([ref[...] for ref in refs], axis=0) if len(refs) > 1 else refs[0][...]


def grad_kernel(n_parts, *refs):
    weights, tokens, outs, acc = refs[:n_parts], refs[n_parts : n_parts + 8], refs[-3:-1], refs[-1]
    step = pl.program_id(0)

    @pl.when(step == 0)
    def _():
        acc[...] = jnp.zeros_like(acc)

    weight = weight_block(weights)
    for place in range(4):
        here = jnp.concatenate([tokens[2 * place][...], tokens[2 * place + 1][...]], axis=0)
        acc[place] += nt(weight, here)

    @pl.when(step == pl.num_programs(0) - 1)
    def _():
        for place in range(4):
            outs[0][place] = acc[place, :, :TILE].astype(BF16)
            outs[1][place] = acc[place, :, TILE:].astype(BF16)


def grad_parts(weights, tokens):
    rows = sum(part.shape[0] for part in weights)
    width = weights[0].shape[1]
    step = 512
    return plain_call(
        functools.partial(grad_kernel, len(weights)),
        (width // step,),
        [pl.BlockSpec((part.shape[0], step), lambda k: (0, k)) for part in (*weights, *tokens)],
        [whole((4, rows, TILE))] * 2,
        [jax.ShapeDtypeStruct((4, rows, TILE), BF16)] * 2,
        [pltpu.VMEM((4, rows, 2 * TILE), F32)],
    )(*in_hbm(weights), *in_hbm(tokens))


def project_kernel(n_parts, core, split, *refs):
    weights, parts, rest = refs[:n_parts], refs[n_parts : n_parts + 4], refs[n_parts + 4 :]
    turned = rest[-1]
    step = pl.program_id(0)

    @pl.when(step == 0)
    def _():
        for place in range(4):
            turned[place * TILE : (place + 1) * TILE, :] = parts[place][core].T

    result = nn(turned[...], weight_block(weights))
    blocks = [result[place * TILE : (place + 1) * TILE] for place in range(4)]
    second = step >= split
    if core:
        out = rest[0]
        for slot, place in enumerate((0, jnp.where(second, 2, 1), jnp.where(second, 1, 2), 3)):
            out[0, place] = blocks[slot].astype(BF16)
    else:
        added, keep, send_first, send_second = rest[:-1]

        def total(place, slot):
            return (blocks[place] + added[0, slot].astype(F32)).astype(BF16)

        @pl.when(step < split)
        def _():
            for slot in range(2):
                keep[0, slot] = total(slot, slot)
                send_first[slot] = total(2 + slot, 2 + slot)

        @pl.when(second)
        def _():
            for slot in range(2):
                keep[0, slot] = total(2 * slot, slot)
                send_second[slot] = total(2 * slot + 1, 2 + slot)


def project(weights, parts, core, added=()):
    rows = sum(part.shape[0] for part in weights)
    width = weights[0].shape[1]
    step = 512
    split = width // 2 // step
    every = pl.BlockSpec((1, 4, TILE, step), lambda j: (j // split, 0, 0, j % split))
    sent = (2, TILE, width // 2)
    near = [
        pl.BlockSpec((1, 2, TILE, step), lambda j: (j // split, 0, 0, j % split)),
        pl.BlockSpec((2, TILE, step), lambda j: (0, 0, jnp.minimum(j, split - 1))),
        pl.BlockSpec((2, TILE, step), lambda j: (0, 0, jnp.maximum(j - split, 0))),
    ]
    return plain_call(
        functools.partial(project_kernel, len(weights), core, split),
        (width // step,),
        [pl.BlockSpec((part.shape[0], step), lambda j: (0, j)) for part in weights]
        + [whole(part.shape) for part in parts]
        + [every] * len(added),
        every if core else near,
        jax.ShapeDtypeStruct((2, 4, TILE, width // 2), BF16)
        if core
        else [jax.ShapeDtypeStruct(shape, BF16) for shape in ((2, *sent), sent, sent)],
        [pltpu.VMEM((4 * TILE, rows), BF16)],
    )(*in_hbm(weights), *parts, *added)


def bias_kernel(shifts, frames, where, bias):
    band_idx, col_idx, frame_idx = where[0], where[1], where[2]
    at = lax.broadcasted_iota(jnp.int32, (SLOT, TILE), 0)
    query = lax.broadcasted_iota(jnp.int32, (SLOT, TILE), 1)
    rim = at - TILE
    outer = jnp.where(band_idx == 0, ROWS, -1)
    row = jnp.where(rim < 0, at // TCOLS, jnp.where(rim < 16, rim % ROWS, outer))
    col = jnp.where(rim < 16, jnp.where(rim < 8, -1, TCOLS), rim - 16)
    col = jnp.where(rim < 0, at % TCOLS, jnp.where(rim < 32, col, (rim - 32) * (TCOLS + 1) - 1))
    across = col_idx * TCOLS + col
    near = (jnp.abs(col - query % TCOLS) <= 1) & (rim < 34)
    near &= (across >= 0) & (across < CTILES * TCOLS)
    gap = jnp.abs(row - query // TCOLS)
    for row_reach in range(2):
        space = jnp.where(near & (gap <= row_reach), 0.0, -1e30)
        for slot, shift in enumerate(shifts):
            there = (frame_idx + shift >= 0) & (frame_idx + shift < frames) | (frames == 2)
            for frame_reach in range(2):
                time = jnp.where(there & (abs(shift) <= frame_reach), 0.0, -1e30)
                bias[2 * frame_reach + row_reach, slot * SLOT : (slot + 1) * SLOT, :] = (
                    jnp.minimum(space, time)
                )


def window_bias(shifts, frames, where):
    shape = (4, len(shifts) * SLOT, TILE)
    return plain_call(
        functools.partial(bias_kernel, shifts, frames),
        (1,),
        [SCALARS],
        whole(shape),
        jax.ShapeDtypeStruct(shape, F32),
        [],
    )(where)


def permute(block, route):
    return lax.ppermute(block, "tensor", route)


def swap(block, group_bit, bits):
    groups, devices = lax.axis_size("groups"), lax.axis_size("tensor")
    return lax.ppermute(
        block,
        ("groups", "tensor"),
        [
            (g * devices + i, (g ^ group_bit) * devices + (i ^ bits))
            for g in range(groups)
            for i in range(devices)
        ],
    )


def after(value, *done):
    return lax.optimization_barrier((value, done))[0]


def exchange(like, other, until):
    pairs = pack(like, swap(other, 0, 1))
    got = [swap(pair, x, 2 * y) for (x, y), pair in zip(PLACES[1:], pairs[1:])]
    return [pairs[0], *after(got, until)]


def on_device(
    input_queries,
    input_keys,
    input_values,
    output_matrix,
    adapter_down_weight,
    adapter_up_weight,
    upstream,
    window_frame_reach,
    window_row_reach,
):
    devices = lax.axis_size("tensor")
    frames = devices // (BANDS * CTILES)
    position = lax.axis_index("tensor")
    frame_idx = position % frames
    col_idx = position // frames % CTILES
    band_idx = position // (frames * CTILES)
    everyone = range(devices)
    to_right = [(i, i + frames) for i in everyone if i // frames % CTILES < CTILES - 1]
    to_left = [(j, i) for i, j in to_right]
    to_band = [(i, (i + devices // BANDS) % devices) for i in everyone]
    if frames == 1:
        shifts, to_frame = [0], []
    elif frames == 2:
        shifts, to_frame = [0, 1], [[(i, i ^ 1) for i in everyone]]
    else:
        later = [(i, i + 1) for i in everyone if i % frames < frames - 1]
        shifts, to_frame = [0, -1, 1], [later, [(j, i) for i, j in later]]
    edge_row = jnp.where(band_idx == 0, ROWS - 1, 0)
    second = position % 2
    combo = jnp.append(2 * window_frame_reach + window_row_reach, second)

    edge_at = edge_row[None]
    leftmost, rightmost, edge = column_call(
        edge_kernel, [edge_at], [input_keys, input_values], [16, 16, 32]
    )
    right = permute(leftmost, to_left)
    left = permute(rightmost, to_right)
    core_slots = [
        (permute(input_keys, route), permute(input_values, route)) for route in to_frame
    ]
    tokens = {(0, 0, 0): upstream, (0, 0, 1): swap(upstream, 0, 1)}
    group = lax.axis_index("groups")
    turns = devices // 4
    me = position * 2 + group
    share = output_matrix.shape[0] // 2
    own = lax.dynamic_slice_in_dim(output_matrix, group * share, share)
    top, low_rows = own[: share // 2], own[share // 2 :]
    bias = window_bias(shifts, frames, jnp.stack([band_idx, col_idx, frame_idx]))
    down = adapter_down_weight.T
    grad_low = (ADAPTER * nt(adapter_up_weight, upstream)).astype(BF16)
    extra = tn(down, grad_low)
    start = (left, right, core_slots, tokens[0, 0, 1], own, top, low_rows)
    start = (*start, bias, grad_low, extra, combo)
    to_outer = column_call(outer_kernel, [edge_at], [after(left, start), right, edge], [40])

    outer = permute(to_outer, to_band)
    for x, y in ((1, 0), (0, 1)):
        tokens[x, y, 0] = swap(after(upstream, to_outer), x, 2 * y)
    opened = (outer, tokens[1, 0, 0], tokens[0, 1, 0])
    if turns == 4:
        one, two = swap(after(own, to_outer), 0, 4), swap(after(top, to_outer), 0, 8)
        opened = (*opened, one, two)
        three = swap(after(two, opened), 0, 4)
        two_low = swap(after(low_rows, opened), 0, 8)
        fetched = [three, two_low]
    else:
        found = {0: own}
        for bit in [1 << b for b in reversed(range(turns.bit_length() - 1))]:
            found |= {t ^ bit: swap(block, 0, 4 * bit) for t, block in found.items()}
        weights = [found[t] for t in range(turns)]
        fetched = []
    tokens[1, 1, 0] = swap(after(tokens[0, 1, 0], opened), 1, 0)
    for x, y in ((1, 0), (0, 1)):
        tokens[x, y, 1] = swap(after(tokens[x, y, 0], opened), 0, 1)
    fetched.append(tokens[1, 1, 0])

    rim = column_call(rim_kernel, [], [after(left, opened), right, outer], [2 * RIM])
    slots = [(input_keys, input_values, rim)] + [
        (*core, permute(rim, route)) for core, route in zip(core_slots, to_frame)
    ]
    att, log_total, grads, low = attend(
        combo,
        after(input_queries, extra, tokens[1, 0, 1], tokens[0, 1, 1]),
        slots,
        bias, down, grad_low, upstream
    )

    att, log_total, grads, low = after((att, log_total, grads, low), fetched)

    att_like, att_other = spread(att, me, turns)
    got = permute(grads[1], [(i, i ^ 1) for i in everyone])
    part = grads[0].astype(F32) + got.astype(F32)

    def add_over(part, bit, until):
        part = part.astype(BF16)
        got = permute(part, [(i, i ^ bit) for i in everyone])
        return part.astype(F32) + after(got, until).astype(F32)

    bits = [1 << b for b in range(1, devices.bit_length() - 1)]
    if turns == 4:
        three_low = swap(after(two_low, att), 0, 4)
        weights = [own, one, two, two_low, three, three_low]
    if share % 16:
        weights = [jnp.concatenate(weights)]
    att_packed = pack(att_like, swap(att_other, 0, 1))
    att_got = [swap(pair, x, 2 * y) for (x, y), pair in zip(PLACES[1:], att_packed[1:])]
    tokens[1, 1, 1] = swap(after(tokens[1, 1, 0], part, att_packed), 0, 1)
    grads_like, grads_other = grad_parts(
        [after(weights[0], att), *weights[1:]], [tokens[m] for m in MEMBERS]
    )
    att_of = [att_packed[0], *after(att_got, grads_like)]
    far = project(weights, att_of, 1)
    near, first, second_half = project(weights, att_of, 0, (swap(far, 0, 1),))
    grads_of = exchange(grads_like, grads_other, near)
    first, second_half = after((first, second_half), grads_of)
    first, second_half = swap(first, 0, 2), swap(second_half, 1, 0)
    over_two, over_one = bits[-1], bits[1:-1]
    part = add_over(after(part, grads_like), over_two, near)
    grads_of[0] = after(grads_of[0], part)
    grad_att = collect(grads_of, me, turns)
    grad_query, terms = attend_back(
        combo, after(input_queries, near), slots, bias, att, grad_att, extra, log_total
    )
    for bit in over_one:
        part = add_over(part, bit, terms)
    grad_query, terms = after((grad_query, terms), first, second_half, part)
    first = near[0].astype(F32) + after(first, grad_query).astype(F32)
    second_half = near[1].astype(F32) + after(second_half, grad_query).astype(F32)
    core, rim_terms = terms[0]
    rim_terms = rim_terms.astype(F32)
    back = [[(j, i) for i, j in route] for route in to_frame]
    for (_, sent), route in zip(terms[1:], back):
        rim_terms += permute(sent, route).astype(F32)
    core_terms = [core] + [permute(sent, route) for (sent, _), route in zip(terms[1:], back)]
    rim_terms = after(rim_terms, core_terms)
    keys_out, values_out = rim_terms[:RIM], rim_terms[RIM:]
    outer = permute(
        jnp.concatenate(
            [keys_out[16:32], values_out[16:32], keys_out[32:34], values_out[32:34]]
        ).astype(BF16),
        to_band,
    )
    part = add_over(part, bits[0], outer)
    last_rows = swap(first[1].astype(BF16), 1, 0), swap(second_half[1].astype(BF16), 0, 2)
    last_rows = after(last_rows, outer)
    outer = after(outer, last_rows)
    first = first[0] + last_rows[0].astype(F32)
    second_half = second_half[0] + last_rows[1].astype(F32)
    projected = (
        jnp.concatenate([first, second_half], axis=1) + ADAPTER * tn(low, adapter_up_weight)
    ).astype(BF16)

    part = part.astype(BF16)
    other = permute(part, [(i, i ^ 1) for i in everyone])
    grad_down = jnp.where(second == 0, part, other).astype(F32).T
    grad_up = jnp.where(second == 0, other, part).astype(F32)

    at_edge = (jnp.arange(ROWS)[:, None] == edge_row).astype(F32)
    outer_corners = outer[32:].astype(F32)

    def side(number):
        at = 8 * number
        return jnp.concatenate(
            [
                keys_out[at : at + 8] + at_edge * outer_corners[number],
                values_out[at : at + 8] + at_edge * outer_corners[2 + number],
            ]
        ).astype(BF16)

    from_right = permute(side(0), to_left)
    from_left = permute(side(1), to_right)
    cell = jnp.arange(TILE, dtype=jnp.int32)
    mark = jnp.arange(32, dtype=jnp.int32)
    source = jnp.where(
        mark < 8,
        mark * TCOLS,
        jnp.where(mark < 16, (mark - 8) * TCOLS + TCOLS - 1, edge_row * TCOLS + mark - 16),
    )
    pick = (source[:, None] == cell[None, :]).astype(BF16)
    gathered = [
        jnp.concatenate([from_left[at : at + 8], from_right[at : at + 8], outer[row : row + 16]])
        for at, row in ((0, 0), (8, 16))
    ]
    grad_key, grad_value = (
        (
            sum(block[rows].astype(F32) for block in core_terms) + tn(pick, got)
        ).astype(BF16)
        for rows, got in ((slice(0, TILE), gathered[0]), (slice(TILE, None), gathered[1]))
    )
    return (projected, grad_query, grad_key, grad_value, grad_down, grad_up)


def solution(mesh):
    tokens = P(("groups", "tensor"), None)
    return jax.shard_map(
        on_device,
        mesh=mesh,
        in_specs=(tokens, tokens, tokens, P("tensor", None), P(), P(), tokens, P(), P()),
        out_specs=(tokens, tokens, tokens, tokens, P("groups", None), P("groups", None)),
        check_vma=False,
    )
```

```python
import functools

import jax
import jax.numpy as jnp
from jax import lax
from jax.experimental import pallas as pl
from jax.experimental.pallas import tpu as pltpu
from jax.sharding import PartitionSpec as P

ROWS = 8
CTILES = 4
BANDS = 2
TCOLS = 16
TILE = ROWS * TCOLS
RIM = 48
SLOT = TILE + RIM
HEAD = 128
STEP = 8

SCALE = HEAD**-0.5
ADAPTER = 0.5
F32 = jnp.float32
BF16 = jnp.bfloat16


def nn(a, b):
    return jnp.dot(a, b, preferred_element_type=F32)


def nt(a, b):
    return lax.dot_general(a, b, (((1,), (1,)), ((), ())), preferred_element_type=F32)


def tn(a, b):
    return lax.dot_general(a, b, (((0,), (0,)), ((), ())), preferred_element_type=F32)


def slot_keys(slots, cols):
    keys, values = [], []
    for core_keys, core_values, rim in slots:
        keys += [core_keys[:, cols], rim[:RIM, cols]]
        values += [core_values[:, cols], rim[RIM:, cols]]
    return jnp.concatenate(keys, axis=0), jnp.concatenate(values, axis=0)


def forward_kernel(n_slots, combo, query, *refs):
    slots = [refs[3 * i : 3 * i + 3] for i in range(n_slots)]
    bias, down, grad_low, upstream, att_ref, log_ref, grads_ref, low_ref, low_acc = refs[
        3 * n_slots :
    ]
    step = pl.program_id(0)
    last = combo.shape[0] - 1

    @pl.when(step == 0)
    def _():
        low_acc[...] = jnp.zeros_like(low_acc)

    columns = [slice(i * HEAD, (i + 1) * HEAD) for i in range(STEP)]
    pairs = [slot_keys(slots, cols) for cols in columns]
    scores = [
        nt(keys, query[:, cols]) * SCALE + bias[combo[step * STEP + i]]
        for i, (cols, (keys, _)) in enumerate(zip(columns, pairs))
    ]
    tops = [jnp.max(block, axis=0, keepdims=True) for block in scores]
    weights = [jnp.exp(block - top) for block, top in zip(scores, tops)]
    totals = [jnp.sum(block, axis=0, keepdims=True) for block in weights]
    mixed = [tn(values, block.astype(BF16)) for (_, values), block in zip(pairs, weights)]
    att = jnp.concatenate(
        [(block * (1.0 / total)).astype(BF16) for block, total in zip(mixed, totals)]
    )
    att_ref[...] = att
    log_ref[0] = jnp.concatenate([top + jnp.log(total) for top, total in zip(tops, totals)])
    low_acc[...] += nn(down[...], att)
    at = pl.ds(pl.multiple_of(step * STEP * HEAD, STEP * HEAD), STEP * HEAD)
    grads_ref[combo[last], :, at] = nt(grad_low[...], att).astype(BF16)

    @pl.when(step == pl.num_programs(0) - 1)
    def _():
        low = low_acc[...].astype(BF16)
        low_ref[...] = low
        grads_ref[1 - combo[last]] = (ADAPTER * nn(low, upstream[...])).astype(BF16)


def backward_kernel(n_slots, combo, query, *refs):
    slots = [refs[3 * i : 3 * i + 3] for i in range(n_slots)]
    bias, att, grad, extra, log_total, grad_query = refs[3 * n_slots : 3 * n_slots + 6]
    terms = refs[3 * n_slots + 6 :]
    step = pl.program_id(0)
    columns = [slice(i * HEAD, (i + 1) * HEAD) for i in range(STEP)]
    pairs = [slot_keys(slots, cols) for cols in columns]
    scores = [
        nt(keys, query[:, cols]) * SCALE + bias[combo[step * STEP + i]]
        for i, (cols, (keys, _)) in enumerate(zip(columns, pairs))
    ]
    grad_att = [(grad[cols, :].astype(F32) + extra[cols, :]).astype(BF16) for cols in columns]
    grad_probs = [nn(values, block) for (_, values), block in zip(pairs, grad_att)]
    inner = [
        jnp.sum(block.astype(F32) * att[cols, :].astype(F32), axis=0, keepdims=True)
        for block, cols in zip(grad_att, columns)
    ]
    probs = [jnp.exp(block - log_total[0, i : i + 1, :]) for i, block in enumerate(scores)]
    grad_scores = [
        (p * (gp - minus)).astype(BF16) for p, gp, minus in zip(probs, grad_probs, inner)
    ]
    for i, cols in enumerate(columns):
        value_terms = nt(probs[i].astype(BF16), grad_att[i]).astype(BF16)
        key_terms = (nn(grad_scores[i], query[:, cols]) * SCALE).astype(BF16)
        grad_query[:, cols] = (tn(grad_scores[i], pairs[i][0]) * SCALE).astype(BF16)
        for s in range(n_slots):
            core, rim = terms[2 * s : 2 * s + 2]
            at = s * SLOT
            core[:TILE, cols] = key_terms[at : at + TILE]
            core[TILE:, cols] = value_terms[at : at + TILE]
            rim[:RIM, cols] = key_terms[at + TILE : at + SLOT]
            rim[RIM:, cols] = value_terms[at + TILE : at + SLOT]


def column_block(rows):
    return pl.BlockSpec((rows, STEP * HEAD), lambda step, *_: (0, step))


def row_block():
    return pl.BlockSpec((STEP * HEAD, TILE), lambda step, *_: (step, 0))


def whole(shape):
    return pl.BlockSpec(shape, lambda *_: (0,) * len(shape))


def head_call(kernel, n_slots, steps, in_specs, out_specs, out_shape, scratch):
    call = pl.pallas_call(
        kernel,
        grid_spec=pltpu.PrefetchScalarGridSpec(
            num_scalar_prefetch=1,
            grid=(steps,),
            in_specs=in_specs,
            out_specs=out_specs,
            scratch_shapes=scratch,
        ),
        out_shape=out_shape,
        compiler_params=pltpu.CompilerParams(
            dimension_semantics=("arbitrary",), vmem_limit_bytes=max(2, n_slots) * 7 * 1024 * 1024
        ),
        cost_estimate=pl.CostEstimate(flops=1000, bytes_accessed=1000, transcendentals=0),
    )

    def from_hbm(scalars, *arrays):
        return call(scalars, *in_hbm(arrays[:3]), *arrays[3:])

    return from_hbm


def in_hbm(arrays):
    return [pltpu.with_memory_space_constraint(array, pltpu.HBM) for array in arrays]


def slot_specs(n_slots):
    return [column_block(TILE), column_block(TILE), column_block(2 * RIM)] * n_slots


def attend(combo, query, slots, bias, down, grad_low, upstream):
    tokens, width = query.shape
    heads = width // HEAD
    rank = down.shape[0]
    n_slots = len(slots)
    return head_call(
        functools.partial(forward_kernel, n_slots),
        n_slots,
        heads // STEP,
        [column_block(tokens)]
        + slot_specs(n_slots)
        + [
            whole(bias.shape),
            column_block(rank),
            whole(grad_low.shape),
            whole(upstream.shape),
        ],
        [
            row_block(),
            pl.BlockSpec((1, STEP, tokens), lambda step, *_: (step, 0, 0)),
            whole((2, rank, width)),
            whole((rank, tokens)),
        ],
        [
            pltpu.HBM((width, tokens), BF16),
            jax.ShapeDtypeStruct((heads // STEP, STEP, tokens), F32),
            jax.ShapeDtypeStruct((2, rank, width), BF16),
            jax.ShapeDtypeStruct((rank, tokens), BF16),
        ],
        [pltpu.VMEM((rank, tokens), F32)],
    )(combo, query, *[part for slot in slots for part in slot], bias, *in_hbm([down]), grad_low, *in_hbm([upstream]))


def attend_back(combo, query, slots, bias, att, grad, extra, log_total):
    tokens, width = query.shape
    heads = width // HEAD
    n_slots = len(slots)
    out = head_call(
        functools.partial(backward_kernel, n_slots),
        n_slots,
        heads // STEP,
        [column_block(tokens)]
        + slot_specs(n_slots)
        + [
            whole(bias.shape),
            row_block(),
            row_block(),
            row_block(),
            pl.BlockSpec((1, STEP, tokens), lambda step, *_: (step, 0, 0)),
        ],
        [column_block(tokens)] + [column_block(2 * TILE), column_block(2 * RIM)] * n_slots,
        [pltpu.HBM((tokens, width), BF16)]
        + [pltpu.HBM((2 * TILE, width), BF16), pltpu.HBM((2 * RIM, width), BF16)] * n_slots,
        [],
    )(
        combo, query, *[part for slot in slots for part in slot], bias, *in_hbm([att]), grad, extra,
        log_total,
    )
    return out[0], [out[1 + 2 * s : 3 + 2 * s] for s in range(n_slots)]


PLACES = [(x, y) for y in range(2) for x in range(2)]
MEMBERS = [(x, y, c) for x, y in PLACES for c in range(2)]


def block_of(member, turn):
    x, y, c = member
    return turn * 8 + y * 4 + c * 2 + x


def plain_call(kernel, grid, in_specs, out_specs, out_shape, scratch):
    return pl.pallas_call(
        kernel,
        grid=grid,
        in_specs=in_specs,
        out_specs=out_specs,
        out_shape=out_shape,
        scratch_shapes=scratch,
        compiler_params=pltpu.CompilerParams(
            dimension_semantics=("arbitrary",) * len(grid), vmem_limit_bytes=14 * 1024 * 1024
        ),
        cost_estimate=pl.CostEstimate(flops=1000, bytes_accessed=1000, transcendentals=0),
    )


def spread_kernel(turns, me, rows_ref, *outs):
    size = rows_ref.shape[0] // (8 * turns)
    for number, member in enumerate(MEMBERS):
        for turn in range(turns):
            at = pl.multiple_of((block_of(member, turn) ^ me[0]) * size, size)
            outs[number % 2][number // 2, turn * size : (turn + 1) * size, :] = rows_ref[
                pl.ds(at, size), :
            ]


def collect_kernel(turns, me, *refs):
    out = refs[-1]
    size = out.shape[0] // (8 * turns)
    for number, member in enumerate(MEMBERS):
        part = refs[number // 2].at[number % 2]
        for turn in range(turns):
            at = pl.multiple_of((block_of(member, turn) ^ me[0]) * size, size)
            out[pl.ds(at, size), :] = part[turn * size : (turn + 1) * size, :]


SCALARS = pl.BlockSpec(memory_space=pltpu.SMEM)


def spread(rows, me, turns):
    total, tokens = rows.shape
    size = total // (8 * turns)
    part = (4, turns * size, tokens)
    if size % 16:
        blocks = rows.reshape(8 * turns, size, tokens)
        order = [[block_of((x, y, c), t) for x, y in PLACES for t in range(turns)] for c in range(2)]
        return [jnp.take(blocks, me ^ jnp.array(o), axis=0).reshape(part) for o in order]
    return plain_call(
        functools.partial(spread_kernel, turns),
        (1,),
        [SCALARS, whole(rows.shape)],
        [whole(part)] * 2,
        [jax.ShapeDtypeStruct(part, rows.dtype)] * 2,
        [],
    )(me[None], *in_hbm([rows]))


def collect(parts, me, turns):
    _, rows, tokens = parts[0].shape
    size = rows // turns
    total = 8 * rows
    if size % 16:
        every = [parts[number // 2][number % 2] for number in range(8)]
        blocks = jnp.concatenate(every).reshape(8 * turns, size, tokens)
        slot = {block_of(m, t): i * turns + t for i, m in enumerate(MEMBERS) for t in range(turns)}
        order = jnp.array([slot[b] for b in range(8 * turns)])
        return jnp.take(blocks, order[me ^ jnp.arange(8 * turns)], axis=0).reshape(total, tokens)
    return plain_call(
        functools.partial(collect_kernel, turns),
        (1,),
        [SCALARS] + [whole(part.shape) for part in parts],
        whole((total, tokens)),
        jax.ShapeDtypeStruct((total, tokens), parts[0].dtype),
        [],
    )(me[None], *in_hbm(parts))


def edge_kernel(where, keys, values, to_left, to_right, edge):
    mark = lax.broadcasted_iota(jnp.int32, (32, TILE), 0)
    cell = lax.broadcasted_iota(jnp.int32, (32, TILE), 1)
    side = jnp.where(mark < 8, mark * TCOLS, (mark - 8) * TCOLS + TCOLS - 1)
    source = jnp.where(mark < 16, side, where[0] * TCOLS + mark - 16)
    pick = (source == cell).astype(F32).astype(BF16)
    key_edges = nn(pick, keys[...])
    value_edges = nn(pick, values[...])
    to_left[...] = jnp.concatenate([key_edges[:8], value_edges[:8]]).astype(BF16)
    to_right[...] = jnp.concatenate([key_edges[8:16], value_edges[8:16]]).astype(BF16)
    edge[...] = jnp.concatenate([key_edges[16:], value_edges[16:]]).astype(BF16)


def outer_kernel(where, left, right, edge, outer):
    sides = [left[...].astype(F32), right[...].astype(F32)]
    last = where[0] == ROWS - 1
    corners = [
        jnp.where(last, side[at + ROWS - 1 : at + ROWS], side[at : at + 1])
        for at in (0, 8)
        for side in sides
    ]
    blank = jnp.zeros((4, edge.shape[1]), F32)
    outer[...] = jnp.concatenate([edge[...].astype(F32), *corners, blank]).astype(BF16)


def rim_kernel(left, right, outer, rim):
    sides = [left[...].astype(F32), right[...].astype(F32)]
    far = outer[...].astype(F32)
    blank = jnp.zeros((14, far.shape[1]), F32)
    rim[...] = jnp.concatenate(
        [
            sides[0][:8], sides[1][:8], far[:16], far[32:34], blank,
            sides[0][8:], sides[1][8:], far[16:32], far[34:36], blank,
        ]
    ).astype(BF16)


def column_call(kernel, scalars, blocks, out_rows, hbm=False):
    width = blocks[0].shape[1]
    step = width // 4
    out = plain_call(
        kernel,
        (4,),
        [SCALARS] * len(scalars)
        + [pl.BlockSpec((block.shape[0], step), lambda j: (0, j)) for block in blocks],
        [pl.BlockSpec((rows, step), lambda j: (0, j)) for rows in out_rows],
        [(pltpu.HBM if hbm else jax.ShapeDtypeStruct)((rows, width), BF16) for rows in out_rows],
        [],
    )(*scalars, *(in_hbm(blocks) if hbm else blocks))
    return out if len(out_rows) > 1 else out[0]


def pack_kernel(here, there, *outs):
    for place, out in enumerate(outs):
        out[0] = here[place]
        out[1] = there[place]


def pack(here, there):
    _, rows, tokens = here.shape
    return plain_call(
        pack_kernel,
        (1,),
        [whole(here.shape)] * 2,
        [whole((2, rows, tokens))] * 4,
        [jax.ShapeDtypeStruct((2, rows, tokens), BF16)] * 4,
        [],
    )(here, there)


def weight_block(refs):
    return jnp.concatenate([ref[...] for ref in refs], axis=0) if len(refs) > 1 else refs[0][...]


def grad_kernel(n_parts, counts, *refs):
    weights, tokens, outs, acc = refs[:n_parts], refs[n_parts:-3], refs[-3:-1], refs[-1]
    step = pl.program_id(0)

    @pl.when(step == 0)
    def _():
        acc[...] = jnp.zeros_like(acc)

    weight = weight_block(weights)
    at = 0
    for place, count in enumerate(counts):
        here = jnp.concatenate([ref[...] for ref in tokens[at : at + count]], axis=0)
        acc[place] += nt(weight, here)
        at += count

    @pl.when(step == pl.num_programs(0) - 1)
    def _():
        for place in range(4):
            outs[0][place] = acc[place, :, :TILE].astype(BF16)
            outs[1][place] = acc[place, :, TILE:].astype(BF16)


def grad_parts(weights, tokens):
    rows = sum(part.shape[0] for part in weights)
    width = weights[0].shape[1]
    step = 1536
    counts = [len(parts) for parts in tokens]
    tokens = [part for parts in tokens for part in parts]
    return plain_call(
        functools.partial(grad_kernel, len(weights), counts),
        (width // step,),
        [pl.BlockSpec((part.shape[0], step), lambda k: (0, k)) for part in (*weights, *tokens)],
        [whole((4, rows, TILE))] * 2,
        [jax.ShapeDtypeStruct((4, rows, TILE), BF16)] * 2,
        [pltpu.VMEM((4, rows, 2 * TILE), F32)],
    )(*in_hbm(weights), *in_hbm(tokens))


def project_kernel(n_parts, core, kept, *refs):
    weights, parts, rest = refs[:n_parts], refs[n_parts : n_parts + 4], refs[n_parts + 4 :]
    turned = rest[-1]

    @pl.when(pl.program_id(0) == 0)
    def _():
        for place in range(4):
            turned[place * TILE : (place + 1) * TILE, :] = parts[place][core].T

    result = nn(turned[...], weight_block(weights))
    blocks = [result[place * TILE : (place + 1) * TILE] for place in range(4)]
    if core:
        for place in range(4):
            rest[0][place] = blocks[place].astype(BF16)
    else:
        added, keep, send = rest[:-1]
        for out, places in ((keep, kept), (send, [p for p in range(4) if p not in kept])):
            for slot, place in enumerate(places):
                out[slot] = (blocks[place] + added[place].astype(F32)).astype(BF16)


def project(weights, parts, core, half, added=()):
    rows = sum(part.shape[0] for part in weights)
    width = weights[0].shape[1] // 2
    step = 768
    split = width // step
    kept = [0, 2] if half else [0, 1]
    four = pl.BlockSpec((4, TILE, step), lambda j: (0, 0, j))
    two = pl.BlockSpec((2, TILE, step), lambda j: (0, 0, j))
    shape = (2, TILE, width)
    return plain_call(
        functools.partial(project_kernel, len(weights), core, kept),
        (split,),
        [pl.BlockSpec((part.shape[0], step), lambda j: (0, half * split + j)) for part in weights]
        + [whole(part.shape) for part in parts]
        + [four] * len(added),
        four if core else [two] * 2,
        jax.ShapeDtypeStruct((4, TILE, width), BF16)
        if core
        else [jax.ShapeDtypeStruct(shape, BF16)] * 2,
        [pltpu.VMEM((4 * TILE, rows), BF16)],
    )(*in_hbm(weights), *in_hbm(parts), *added)


def bias_kernel(shifts, frames, where, bias):
    band_idx, col_idx, frame_idx = where[0], where[1], where[2]
    at = lax.broadcasted_iota(jnp.int32, (SLOT, TILE), 0)
    query = lax.broadcasted_iota(jnp.int32, (SLOT, TILE), 1)
    rim = at - TILE
    outer = jnp.where(band_idx == 0, ROWS, -1)
    row = jnp.where(rim < 0, at // TCOLS, jnp.where(rim < 16, rim % ROWS, outer))
    col = jnp.where(rim < 16, jnp.where(rim < 8, -1, TCOLS), rim - 16)
    col = jnp.where(rim < 0, at % TCOLS, jnp.where(rim < 32, col, (rim - 32) * (TCOLS + 1) - 1))
    across = col_idx * TCOLS + col
    near = (jnp.abs(col - query % TCOLS) <= 1) & (rim < 34)
    near &= (across >= 0) & (across < CTILES * TCOLS)
    gap = jnp.abs(row - query // TCOLS)
    for row_reach in range(2):
        space = jnp.where(near & (gap <= row_reach), 0.0, -1e30)
        for slot, shift in enumerate(shifts):
            there = (frame_idx + shift >= 0) & (frame_idx + shift < frames) | (frames == 2)
            for frame_reach in range(2):
                time = jnp.where(there & (abs(shift) <= frame_reach), 0.0, -1e30)
                bias[2 * frame_reach + row_reach, slot * SLOT : (slot + 1) * SLOT, :] = (
                    jnp.minimum(space, time)
                )


def window_bias(shifts, frames, where):
    shape = (4, len(shifts) * SLOT, TILE)
    return plain_call(
        functools.partial(bias_kernel, shifts, frames),
        (1,),
        [SCALARS],
        whole(shape),
        jax.ShapeDtypeStruct(shape, F32),
        [],
    )(where)


def permute(block, route):
    return lax.ppermute(block, "tensor", route)


def swap(block, group_bit, bits):
    groups, devices = lax.axis_size("groups"), lax.axis_size("tensor")
    return lax.ppermute(
        block,
        ("groups", "tensor"),
        [
            (g * devices + i, (g ^ group_bit) * devices + (i ^ bits))
            for g in range(groups)
            for i in range(devices)
        ],
    )


def after(value, *done):
    return lax.optimization_barrier((value, done))[0]


def on_device(
    input_queries,
    input_keys,
    input_values,
    output_matrix,
    adapter_down_weight,
    adapter_up_weight,
    upstream,
    window_frame_reach,
    window_row_reach,
):
    devices = lax.axis_size("tensor")
    frames = devices // (BANDS * CTILES)
    position = lax.axis_index("tensor")
    frame_idx = position % frames
    col_idx = position // frames % CTILES
    band_idx = position // (frames * CTILES)
    everyone = range(devices)
    to_right = [(i, i + frames) for i in everyone if i // frames % CTILES < CTILES - 1]
    to_left = [(j, i) for i, j in to_right]
    to_band = [(i, (i + devices // BANDS) % devices) for i in everyone]
    if frames == 1:
        shifts, to_frame = [0], []
    elif frames == 2:
        shifts, to_frame = [0, 1], [[(i, i ^ 1) for i in everyone]]
    else:
        later = [(i, i + 1) for i in everyone if i % frames < frames - 1]
        shifts, to_frame = [0, -1, 1], [later, [(j, i) for i, j in later]]
    edge_row = jnp.where(band_idx == 0, ROWS - 1, 0)
    second = position % 2
    combo = jnp.append(2 * window_frame_reach + window_row_reach, second)

    edge_at = edge_row[None]
    leftmost, rightmost, edge = column_call(
        edge_kernel, [edge_at], [input_keys, input_values], [16, 16, 32], hbm=True
    )
    core_slots = [
        (permute(input_keys, route), permute(input_values, route)) for route in to_frame
    ]
    leftmost, rightmost = after((leftmost, rightmost), core_slots)
    right = permute(leftmost, to_left)
    left = permute(rightmost, to_right)
    group = lax.axis_index("groups")
    turns = devices // 4
    me = position * 2 + group
    share = output_matrix.shape[0] // 2
    own = lax.dynamic_slice_in_dim(output_matrix, group * share, share)
    top, low_rows = own[: share // 2], own[share // 2 :]
    bias = window_bias(shifts, frames, jnp.stack([band_idx, col_idx, frame_idx]))
    down = adapter_down_weight.T
    grad_low = (ADAPTER * nt(adapter_up_weight, upstream)).astype(BF16)
    extra = tn(down, grad_low)
    across = swap(after(upstream, edge), 1, 0)
    start = [left, right, own, low_rows, bias, grad_low, extra, combo, across, core_slots]
    if turns == 4:
        one, two = swap(after(own, edge), 0, 4), swap(after(top, edge), 0, 8)
        start += [one, two]
    to_outer = column_call(outer_kernel, [edge_at], [after(left, start), right, edge], [40])

    outer = permute(to_outer, to_band)
    beside = swap(after(upstream, to_outer), 0, 2)
    upper = swap(after(across[: TILE // 2], to_outer), 0, 2)
    opened = (outer, beside, upper)
    if turns == 4:
        two_low = swap(after(low_rows, to_outer), 0, 8)
        three = swap(after(two, to_outer), 0, 4)
        opened = (*opened, two_low, three)
        three_low = swap(after(two_low, opened), 0, 4)
        weights = [own, one, two, two_low, three, three_low]
        fetched = [three_low]
    else:
        found = {0: own}
        for bit in [1 << b for b in reversed(range(turns.bit_length() - 1))]:
            found |= {t ^ bit: swap(block, 0, 4 * bit) for t, block in found.items()}
        weights = [found[t] for t in range(turns)]
        fetched = []
    lower = swap(after(beside[TILE // 2 :], opened), 1, 0)
    across_other = swap(after(across, opened), 0, 1)
    fetched.append(lower)

    rim = column_call(rim_kernel, [], [after(left, opened), right, outer], [2 * RIM])
    slots = [(input_keys, input_values, rim)] + [
        (*core, permute(rim, route)) for core, route in zip(core_slots, to_frame)
    ]
    att, log_total, grads, low = attend(
        combo,
        after(input_queries, extra, across_other),
        slots,
        bias, down, grad_low, upstream
    )

    att, log_total, grads, low = after((att, log_total, grads, low), fetched)

    att_like, att_other = spread(att, me, turns)
    got = permute(grads[1], [(i, i ^ 1) for i in everyone])
    part = grads[0].astype(F32) + got.astype(F32)

    def add_over(part, bit, until):
        part = part.astype(BF16)
        got = after(permute(part, [(i, i ^ bit) for i in everyone]), until)
        return part.astype(F32) + got.astype(F32), got

    bits = [1 << b for b in range(1, devices.bit_length() - 1)]
    if share % 16:
        weights = [jnp.concatenate(weights)]
    att_packed = pack(att_like, swap(att_other, 0, 1))
    att_got = [swap(pair, x, 2 * y) for (x, y), pair in zip(PLACES[1:], att_packed[1:])]
    tokens = [
        [upstream, swap(after(upstream, att), 0, 1)],
        [across, across_other],
        [beside, swap(after(beside, att), 0, 1)],
        [upper, lower, swap(after(upper, att), 0, 1), swap(after(lower, att), 0, 1)],
    ]
    grads_like, grads_other = grad_parts([after(weights[0], att), *weights[1:]], tokens)
    att_of = [att_packed[0], *after(att_got, grads_like)]
    for bit in bits[1:-1]:
        part, got = add_over(part, bit, grads_like)
    grads_packed = pack(grads_like, swap(after(grads_other, att_of), 0, 1))
    grads_got = [swap(pair, x, 2 * y) for (x, y), pair in zip(PLACES[1:], grads_packed[1:])]
    near, sent = [], []
    for half in range(2):
        far = swap(after(project(weights, att_of, 1, half), grads_packed, got), 0, 1)
        keep, send = project(weights, att_of, 0, half, (far,))
        near.append(keep)
        sent.append(swap(send, 1, 0) if half else swap(send, 0, 2))
    grads_of = [grads_packed[0], *after(grads_got, near)]
    part, got = add_over(after(part, grads_of), bits[-1], near)
    grad_att = collect(grads_of, me, turns)
    grad_query, terms = attend_back(
        combo, after(input_queries, near), slots, bias, att, grad_att, extra, log_total
    )
    grad_query, terms = after((grad_query, terms), sent, got)
    core, rim_terms = terms[0]
    rim_terms = rim_terms.astype(F32)
    back = [[(j, i) for i, j in route] for route in to_frame]
    for (_, block), route in zip(terms[1:], back):
        rim_terms += permute(block, route).astype(F32)
    core_terms = [core] + [
        permute(after(block, rim_terms), route) for (block, _), route in zip(terms[1:], back)
    ]
    keys_out, values_out = rim_terms[:RIM], rim_terms[RIM:]
    to_outer = jnp.concatenate(
        [keys_out[16:32], values_out[16:32], keys_out[32:34], values_out[32:34]]
    ).astype(BF16)
    outer = permute(to_outer, to_band)
    sent = after(sent, to_outer)
    first, second_half = (
        keep.astype(F32) + block.astype(F32) for keep, block in zip(near, sent)
    )
    part, _ = add_over(part, bits[0], outer)
    last_rows = swap(first[1].astype(BF16), 1, 0), swap(second_half[1].astype(BF16), 0, 2)
    at_edge = (jnp.arange(ROWS)[:, None] == edge_row).astype(F32)
    outer_corners = outer[32:].astype(F32)

    def side(number):
        at = 8 * number
        return jnp.concatenate(
            [
                keys_out[at : at + 8] + at_edge * outer_corners[number],
                values_out[at : at + 8] + at_edge * outer_corners[2 + number],
            ]
        ).astype(BF16)

    sides = side(0), side(1)
    from_right = permute(sides[0], to_left)
    from_left = permute(sides[1], to_right)
    last_rows = after(last_rows, sides)
    first = first[0] + last_rows[0].astype(F32)
    second_half = second_half[0] + last_rows[1].astype(F32)
    projected = (
        jnp.concatenate([first, second_half], axis=1) + ADAPTER * tn(low, adapter_up_weight)
    ).astype(BF16)

    part = after(part.astype(BF16), last_rows)
    other = after(permute(part, [(i, i ^ 1) for i in everyone]), sides)
    grad_down = jnp.where(second == 0, part, other).astype(F32).T
    grad_up = jnp.where(second == 0, other, part).astype(F32)

    from_left, from_right = after((from_left, from_right), projected, grad_down, grad_up)
    cell = jnp.arange(TILE, dtype=jnp.int32)
    mark = jnp.arange(32, dtype=jnp.int32)
    source = jnp.where(
        mark < 8,
        mark * TCOLS,
        jnp.where(mark < 16, (mark - 8) * TCOLS + TCOLS - 1, edge_row * TCOLS + mark - 16),
    )
    pick = (source[:, None] == cell[None, :]).astype(BF16)
    gathered = [
        jnp.concatenate([from_left[at : at + 8], from_right[at : at + 8], outer[row : row + 16]])
        for at, row in ((0, 0), (8, 16))
    ]
    grad_key, grad_value = (
        (
            sum(block[rows].astype(F32) for block in core_terms) + tn(pick, got)
        ).astype(BF16)
        for rows, got in ((slice(0, TILE), gathered[0]), (slice(TILE, None), gathered[1]))
    )
    return (projected, grad_query, grad_key, grad_value, grad_down, grad_up)


def solution(mesh):
    tokens = P(("groups", "tensor"), None)
    return jax.shard_map(
        on_device,
        mesh=mesh,
        in_specs=(tokens, tokens, tokens, P("tensor", None), P(), P(), tokens, P(), P()),
        out_specs=(tokens, tokens, tokens, tokens, P("groups", None), P("groups", None)),
        check_vma=False,
    )
```

```python
import functools

import jax
import jax.numpy as jnp
from jax import lax
from jax.experimental import pallas as pl
from jax.experimental.pallas import tpu as pltpu
from jax.sharding import PartitionSpec as P

ROWS = 8
CTILES = 4
BANDS = 2
TCOLS = 16
TILE = ROWS * TCOLS
RIM = 48
SLOT = TILE + RIM
HEAD = 128
STEP = 8

SCALE = HEAD**-0.5
ADAPTER = 0.5
F32 = jnp.float32
BF16 = jnp.bfloat16


def nn(a, b):
    return jnp.dot(a, b, preferred_element_type=F32)


def nt(a, b):
    return lax.dot_general(a, b, (((1,), (1,)), ((), ())), preferred_element_type=F32)


def tn(a, b):
    return lax.dot_general(a, b, (((0,), (0,)), ((), ())), preferred_element_type=F32)


def slot_keys(slots, cols):
    keys, values = [], []
    for core_keys, core_values, rim in slots:
        keys += [core_keys[:, cols], rim[:RIM, cols]]
        values += [core_values[:, cols], rim[RIM:, cols]]
    return jnp.concatenate(keys, axis=0), jnp.concatenate(values, axis=0)


def forward_kernel(n_slots, turns, combo, query, *refs):
    slots = [refs[3 * i : 3 * i + 3] for i in range(n_slots)]
    bias, down, grad_low, upstream, att_ref, log_ref, grads_ref, low_ref = refs[
        3 * n_slots : 3 * n_slots + 8
    ]
    low_acc, members = refs[-1], refs[3 * n_slots + 8 : -1]
    step = pl.program_id(0)
    second = combo.shape[0] - 2

    @pl.when(step == 0)
    def _():
        low_acc[...] = jnp.zeros_like(low_acc)

    columns = [slice(i * HEAD, (i + 1) * HEAD) for i in range(STEP)]
    pairs = [slot_keys(slots, cols) for cols in columns]
    scores = [
        nt(keys, query[:, cols]) * SCALE + bias[combo[step * STEP + i]]
        for i, (cols, (keys, _)) in enumerate(zip(columns, pairs))
    ]
    tops = [jnp.max(block, axis=0, keepdims=True) for block in scores]
    weights = [jnp.exp(block - top) for block, top in zip(scores, tops)]
    totals = [jnp.sum(block, axis=0, keepdims=True) for block in weights]
    mixed = [tn(values, block.astype(BF16)) for (_, values), block in zip(pairs, weights)]
    att = jnp.concatenate(
        [(block * (1.0 / total)).astype(BF16) for block, total in zip(mixed, totals)]
    )
    att_ref[...] = att
    if members:
        rows = STEP * HEAD
        members[2][pl.ds(pl.multiple_of(step * rows, rows), rows), :] = att
    log_ref[0] = jnp.concatenate([top + jnp.log(total) for top, total in zip(tops, totals)])
    low_acc[...] += nn(down[...], att)
    at = pl.ds(pl.multiple_of(step * STEP * HEAD, STEP * HEAD), STEP * HEAD)
    grads_ref[combo[second], :, at] = nt(grad_low[...], att).astype(BF16)

    @pl.when(step == pl.num_programs(0) - 1)
    def _():
        low = low_acc[...].astype(BF16)
        low_ref[...] = low
        if members:
            spread_kernel(turns, combo[second + 1], members[2], *members[:2])
        grads_ref[1 - combo[second]] = (ADAPTER * nn(low, upstream[...])).astype(BF16)


def backward_kernel(n_slots, combo, query, *refs):
    slots = [refs[3 * i : 3 * i + 3] for i in range(n_slots)]
    bias, att, grad, extra, log_total, grad_query = refs[3 * n_slots : 3 * n_slots + 6]
    terms = refs[3 * n_slots + 6 :]
    step = pl.program_id(0)
    columns = [slice(i * HEAD, (i + 1) * HEAD) for i in range(STEP)]
    pairs = [slot_keys(slots, cols) for cols in columns]
    scores = [
        nt(keys, query[:, cols]) * SCALE + bias[combo[step * STEP + i]]
        for i, (cols, (keys, _)) in enumerate(zip(columns, pairs))
    ]
    grad_att = [(grad[cols, :].astype(F32) + extra[cols, :]).astype(BF16) for cols in columns]
    grad_probs = [nn(values, block) for (_, values), block in zip(pairs, grad_att)]
    inner = [
        jnp.sum(block.astype(F32) * att[cols, :].astype(F32), axis=0, keepdims=True)
        for block, cols in zip(grad_att, columns)
    ]
    probs = [jnp.exp(block - log_total[0, i : i + 1, :]) for i, block in enumerate(scores)]
    grad_scores = [
        (p * (gp - minus)).astype(BF16) for p, gp, minus in zip(probs, grad_probs, inner)
    ]
    for i, cols in enumerate(columns):
        value_terms = nt(probs[i].astype(BF16), grad_att[i]).astype(BF16)
        key_terms = (nn(grad_scores[i], query[:, cols]) * SCALE).astype(BF16)
        grad_query[:, cols] = (tn(grad_scores[i], pairs[i][0]) * SCALE).astype(BF16)
        for s in range(n_slots):
            core, rim = terms[2 * s : 2 * s + 2]
            at = s * SLOT
            core[:TILE, cols] = key_terms[at : at + TILE]
            core[TILE:, cols] = value_terms[at : at + TILE]
            rim[:RIM, cols] = key_terms[at + TILE : at + SLOT]
            rim[RIM:, cols] = value_terms[at + TILE : at + SLOT]


def column_block(rows):
    return pl.BlockSpec((rows, STEP * HEAD), lambda step, *_: (0, step))


def row_block():
    return pl.BlockSpec((STEP * HEAD, TILE), lambda step, *_: (step, 0))


def whole(shape):
    return pl.BlockSpec(shape, lambda *_: (0,) * len(shape))


def head_call(kernel, n_slots, steps, in_specs, out_specs, out_shape, scratch):
    call = pl.pallas_call(
        kernel,
        grid_spec=pltpu.PrefetchScalarGridSpec(
            num_scalar_prefetch=1,
            grid=(steps,),
            in_specs=in_specs,
            out_specs=out_specs,
            scratch_shapes=scratch,
        ),
        out_shape=out_shape,
        compiler_params=pltpu.CompilerParams(
            dimension_semantics=("arbitrary",), vmem_limit_bytes=max(2, n_slots) * 7 * 1024 * 1024
        ),
        cost_estimate=pl.CostEstimate(flops=1000, bytes_accessed=1000, transcendentals=0),
    )

    def from_hbm(scalars, *arrays):
        return call(scalars, *in_hbm(arrays[:3]), *arrays[3:])

    return from_hbm


def in_hbm(arrays):
    return [pltpu.with_memory_space_constraint(array, pltpu.HBM) for array in arrays]


def slot_specs(n_slots):
    return [column_block(TILE), column_block(TILE), column_block(2 * RIM)] * n_slots


def attend(combo, query, slots, bias, down, grad_low, upstream, turns):
    tokens, width = query.shape
    heads = width // HEAD
    rank = down.shape[0]
    n_slots = len(slots)
    aligned = width // (8 * turns) % 16 == 0
    member = (4, width // 8, tokens)
    return head_call(
        functools.partial(forward_kernel, n_slots, turns),
        n_slots,
        heads // STEP,
        [column_block(tokens)]
        + slot_specs(n_slots)
        + [
            whole(bias.shape),
            column_block(rank),
            whole(grad_low.shape),
            whole(upstream.shape),
        ],
        [
            row_block(),
            pl.BlockSpec((1, STEP, tokens), lambda step, *_: (step, 0, 0)),
            whole((2, rank, width)),
            whole((rank, tokens)),
        ]
        + [whole(member)] * 2 * aligned,
        [
            pltpu.HBM((width, tokens), BF16),
            jax.ShapeDtypeStruct((heads // STEP, STEP, tokens), F32),
            jax.ShapeDtypeStruct((2, rank, width), BF16),
            jax.ShapeDtypeStruct((rank, tokens), BF16),
        ]
        + [jax.ShapeDtypeStruct(member, BF16)] * 2 * aligned,
        [pltpu.VMEM((width, tokens), BF16)] * aligned + [pltpu.VMEM((rank, tokens), F32)],
    )(
        combo, query, *[part for slot in slots for part in slot], bias, *in_hbm([down]), grad_low,
        *in_hbm([upstream]),
    )


def attend_back(combo, query, slots, bias, att, grad, extra, log_total):
    tokens, width = query.shape
    heads = width // HEAD
    n_slots = len(slots)
    out = head_call(
        functools.partial(backward_kernel, n_slots),
        n_slots,
        heads // STEP,
        [column_block(tokens)]
        + slot_specs(n_slots)
        + [
            whole(bias.shape),
            row_block(),
            row_block(),
            row_block(),
            pl.BlockSpec((1, STEP, tokens), lambda step, *_: (step, 0, 0)),
        ],
        [column_block(tokens)] + [column_block(2 * TILE), column_block(2 * RIM)] * n_slots,
        [pltpu.HBM((tokens, width), BF16)]
        + [pltpu.HBM((2 * TILE, width), BF16), pltpu.HBM((2 * RIM, width), BF16)] * n_slots,
        [],
    )(
        combo, query, *[part for slot in slots for part in slot], bias, *in_hbm([att]), grad, extra,
        log_total,
    )
    return out[0], [out[1 + 2 * s : 3 + 2 * s] for s in range(n_slots)]


PLACES = [(x, y) for y in range(2) for x in range(2)]
MEMBERS = [(x, y, c) for x, y in PLACES for c in range(2)]


def block_of(member, turn):
    x, y, c = member
    return turn * 8 + y * 4 + c * 2 + x


def plain_call(kernel, grid, in_specs, out_specs, out_shape, scratch):
    return pl.pallas_call(
        kernel,
        grid=grid,
        in_specs=in_specs,
        out_specs=out_specs,
        out_shape=out_shape,
        scratch_shapes=scratch,
        compiler_params=pltpu.CompilerParams(
            dimension_semantics=("arbitrary",) * len(grid), vmem_limit_bytes=14 * 1024 * 1024
        ),
        cost_estimate=pl.CostEstimate(flops=1000, bytes_accessed=1000, transcendentals=0),
    )


def spread_kernel(turns, me, rows_ref, *outs):
    size = rows_ref.shape[0] // (8 * turns)
    for number, member in enumerate(MEMBERS):
        for turn in range(turns):
            at = pl.multiple_of((block_of(member, turn) ^ me) * size, size)
            outs[number % 2][number // 2, turn * size : (turn + 1) * size, :] = rows_ref[
                pl.ds(at, size), :
            ]


def collect_kernel(turns, me, *refs):
    out = refs[-1]
    size = out.shape[0] // (8 * turns)
    for number, member in enumerate(MEMBERS):
        part = refs[number // 2].at[number % 2]
        for turn in range(turns):
            at = pl.multiple_of((block_of(member, turn) ^ me[0]) * size, size)
            out[pl.ds(at, size), :] = part[turn * size : (turn + 1) * size, :]


SCALARS = pl.BlockSpec(memory_space=pltpu.SMEM)


def spread(rows, me, turns):
    total, tokens = rows.shape
    size = total // (8 * turns)
    blocks = rows.reshape(8 * turns, size, tokens)
    order = [[block_of((x, y, c), t) for x, y in PLACES for t in range(turns)] for c in range(2)]
    return [
        jnp.take(blocks, me ^ jnp.array(o), axis=0).reshape(4, turns * size, tokens) for o in order
    ]


def collect(parts, me, turns):
    _, rows, tokens = parts[0].shape
    size = rows // turns
    total = 8 * rows
    if size % 16:
        every = [parts[number // 2][number % 2] for number in range(8)]
        blocks = jnp.concatenate(every).reshape(8 * turns, size, tokens)
        slot = {block_of(m, t): i * turns + t for i, m in enumerate(MEMBERS) for t in range(turns)}
        order = jnp.array([slot[b] for b in range(8 * turns)])
        return jnp.take(blocks, order[me ^ jnp.arange(8 * turns)], axis=0).reshape(total, tokens)
    return plain_call(
        functools.partial(collect_kernel, turns),
        (1,),
        [SCALARS] + [whole(part.shape) for part in parts],
        whole((total, tokens)),
        jax.ShapeDtypeStruct((total, tokens), parts[0].dtype),
        [],
    )(me[None], *in_hbm(parts))


def edge_kernel(where, keys, values, to_left, to_right, edge):
    mark = lax.broadcasted_iota(jnp.int32, (32, TILE), 0)
    cell = lax.broadcasted_iota(jnp.int32, (32, TILE), 1)
    side = jnp.where(mark < 8, mark * TCOLS, (mark - 8) * TCOLS + TCOLS - 1)
    source = jnp.where(mark < 16, side, where[0] * TCOLS + mark - 16)
    pick = (source == cell).astype(F32).astype(BF16)
    key_edges = nn(pick, keys[...])
    value_edges = nn(pick, values[...])
    to_left[...] = jnp.concatenate([key_edges[:8], value_edges[:8]]).astype(BF16)
    to_right[...] = jnp.concatenate([key_edges[8:16], value_edges[8:16]]).astype(BF16)
    edge[...] = jnp.concatenate([key_edges[16:], value_edges[16:]]).astype(BF16)


def outer_kernel(where, left, right, edge, outer):
    sides = [left[...].astype(F32), right[...].astype(F32)]
    last = where[0] == ROWS - 1
    corners = [
        jnp.where(last, side[at + ROWS - 1 : at + ROWS], side[at : at + 1])
        for at in (0, 8)
        for side in sides
    ]
    blank = jnp.zeros((4, edge.shape[1]), F32)
    outer[...] = jnp.concatenate([edge[...].astype(F32), *corners, blank]).astype(BF16)


def rim_kernel(left, right, outer, rim):
    sides = [left[...].astype(F32), right[...].astype(F32)]
    far = outer[...].astype(F32)
    blank = jnp.zeros((14, far.shape[1]), F32)
    rim[...] = jnp.concatenate(
        [
            sides[0][:8], sides[1][:8], far[:16], far[32:34], blank,
            sides[0][8:], sides[1][8:], far[16:32], far[34:36], blank,
        ]
    ).astype(BF16)


def column_call(kernel, scalars, blocks, out_rows, hbm=False):
    width = blocks[0].shape[1]
    step = width // 4
    out = plain_call(
        kernel,
        (4,),
        [SCALARS] * len(scalars)
        + [pl.BlockSpec((block.shape[0], step), lambda j: (0, j)) for block in blocks],
        [pl.BlockSpec((rows, step), lambda j: (0, j)) for rows in out_rows],
        [(pltpu.HBM if hbm else jax.ShapeDtypeStruct)((rows, width), BF16) for rows in out_rows],
        [],
    )(*scalars, *(in_hbm(blocks) if hbm else blocks))
    return out if len(out_rows) > 1 else out[0]


def pack_kernel(here, there, *outs):
    for place, out in enumerate(outs):
        out[0] = here[place]
        out[1] = there[place]


def pack(here, there):
    _, rows, tokens = here.shape
    return plain_call(
        pack_kernel,
        (1,),
        [whole(here.shape)] * 2,
        [whole((2, rows, tokens))] * 4,
        [jax.ShapeDtypeStruct((2, rows, tokens), BF16)] * 4,
        [],
    )(here, there)


def weight_block(refs):
    return jnp.concatenate([ref[...] for ref in refs], axis=0) if len(refs) > 1 else refs[0][...]


def grad_kernel(n_parts, counts, *refs):
    weights, tokens, outs, acc = refs[:n_parts], refs[n_parts:-3], refs[-3:-1], refs[-1]
    step = pl.program_id(0)

    @pl.when(step == 0)
    def _():
        acc[...] = jnp.zeros_like(acc)

    weight = weight_block(weights)
    at = 0
    for place, count in enumerate(counts):
        here = jnp.concatenate([ref[...] for ref in tokens[at : at + count]], axis=0)
        acc[place] += nt(weight, here)
        at += count

    @pl.when(step == pl.num_programs(0) - 1)
    def _():
        for place in range(4):
            outs[0][place] = acc[place, :, :TILE].astype(BF16)
            outs[1][place] = acc[place, :, TILE:].astype(BF16)


def grad_parts(weights, tokens):
    rows = sum(part.shape[0] for part in weights)
    width = weights[0].shape[1]
    step = 1536
    counts = [len(parts) for parts in tokens]
    tokens = [part for parts in tokens for part in parts]
    return plain_call(
        functools.partial(grad_kernel, len(weights), counts),
        (width // step,),
        [pl.BlockSpec((part.shape[0], step), lambda k: (0, k)) for part in (*weights, *tokens)],
        [whole((4, rows, TILE))] * 2,
        [jax.ShapeDtypeStruct((4, rows, TILE), BF16)] * 2,
        [pltpu.VMEM((4, rows, 2 * TILE), F32)],
    )(*in_hbm(weights), *tokens)


def project_kernel(n_parts, core, kept, *refs):
    weights, parts, rest = refs[:n_parts], refs[n_parts : n_parts + 4], refs[n_parts + 4 :]
    turned = rest[-1]

    @pl.when(pl.program_id(0) == 0)
    def _():
        for place in range(4):
            turned[place * TILE : (place + 1) * TILE, :] = parts[place][core].T

    result = nn(turned[...], weight_block(weights))
    blocks = [result[place * TILE : (place + 1) * TILE] for place in range(4)]
    if core:
        for place in range(4):
            rest[0][place] = blocks[place].astype(BF16)
    else:
        added, keep, send = rest[:-1]
        for out, places in ((keep, kept), (send, [p for p in range(4) if p not in kept])):
            for slot, place in enumerate(places):
                out[slot] = (blocks[place] + added[place].astype(F32)).astype(BF16)


def project(weights, parts, core, half, added=()):
    rows = sum(part.shape[0] for part in weights)
    width = weights[0].shape[1] // 2
    step = 768
    split = width // step
    kept = [0, 2] if half else [0, 1]
    four = pl.BlockSpec((4, TILE, step), lambda j: (0, 0, j))
    two = pl.BlockSpec((2, TILE, step), lambda j: (0, 0, j))
    shape = (2, TILE, width)
    return plain_call(
        functools.partial(project_kernel, len(weights), core, kept),
        (split,),
        [pl.BlockSpec((part.shape[0], step), lambda j: (0, half * split + j)) for part in weights]
        + [whole(part.shape) for part in parts]
        + [four] * len(added),
        four if core else [two] * 2,
        jax.ShapeDtypeStruct((4, TILE, width), BF16)
        if core
        else [jax.ShapeDtypeStruct(shape, BF16)] * 2,
        [pltpu.VMEM((4 * TILE, rows), BF16)],
    )(*in_hbm(weights), *in_hbm(parts), *added)


def bias_kernel(shifts, frames, where, bias):
    band_idx, col_idx, frame_idx = where[0], where[1], where[2]
    at = lax.broadcasted_iota(jnp.int32, (SLOT, TILE), 0)
    query = lax.broadcasted_iota(jnp.int32, (SLOT, TILE), 1)
    rim = at - TILE
    outer = jnp.where(band_idx == 0, ROWS, -1)
    row = jnp.where(rim < 0, at // TCOLS, jnp.where(rim < 16, rim % ROWS, outer))
    col = jnp.where(rim < 16, jnp.where(rim < 8, -1, TCOLS), rim - 16)
    col = jnp.where(rim < 0, at % TCOLS, jnp.where(rim < 32, col, (rim - 32) * (TCOLS + 1) - 1))
    across = col_idx * TCOLS + col
    near = (jnp.abs(col - query % TCOLS) <= 1) & (rim < 34)
    near &= (across >= 0) & (across < CTILES * TCOLS)
    gap = jnp.abs(row - query // TCOLS)
    for row_reach in range(2):
        space = jnp.where(near & (gap <= row_reach), 0.0, -1e30)
        for slot, shift in enumerate(shifts):
            there = (frame_idx + shift >= 0) & (frame_idx + shift < frames) | (frames == 2)
            for frame_reach in range(2):
                time = jnp.where(there & (abs(shift) <= frame_reach), 0.0, -1e30)
                bias[2 * frame_reach + row_reach, slot * SLOT : (slot + 1) * SLOT, :] = (
                    jnp.minimum(space, time)
                )


def window_bias(shifts, frames, where):
    shape = (4, len(shifts) * SLOT, TILE)
    return plain_call(
        functools.partial(bias_kernel, shifts, frames),
        (1,),
        [SCALARS],
        whole(shape),
        jax.ShapeDtypeStruct(shape, F32),
        [],
    )(where)


def permute(block, route):
    return lax.ppermute(block, "tensor", route)


def swap(block, group_bit, bits):
    groups, devices = lax.axis_size("groups"), lax.axis_size("tensor")
    return lax.ppermute(
        block,
        ("groups", "tensor"),
        [
            (g * devices + i, (g ^ group_bit) * devices + (i ^ bits))
            for g in range(groups)
            for i in range(devices)
        ],
    )


def after(value, *done):
    return lax.optimization_barrier((value, done))[0]


def on_device(
    input_queries,
    input_keys,
    input_values,
    output_matrix,
    adapter_down_weight,
    adapter_up_weight,
    upstream,
    window_frame_reach,
    window_row_reach,
):
    devices = lax.axis_size("tensor")
    frames = devices // (BANDS * CTILES)
    position = lax.axis_index("tensor")
    frame_idx = position % frames
    col_idx = position // frames % CTILES
    band_idx = position // (frames * CTILES)
    everyone = range(devices)
    to_right = [(i, i + frames) for i in everyone if i // frames % CTILES < CTILES - 1]
    to_left = [(j, i) for i, j in to_right]
    to_band = [(i, (i + devices // BANDS) % devices) for i in everyone]
    if frames == 1:
        shifts, to_frame = [0], []
    elif frames == 2:
        shifts, to_frame = [0, 1], [[(i, i ^ 1) for i in everyone]]
    else:
        later = [(i, i + 1) for i in everyone if i % frames < frames - 1]
        shifts, to_frame = [0, -1, 1], [later, [(j, i) for i, j in later]]
    edge_row = jnp.where(band_idx == 0, ROWS - 1, 0)
    second = position % 2
    me = position * 2 + lax.axis_index("groups")
    combo = jnp.append(2 * window_frame_reach + window_row_reach, jnp.stack([second, me]))

    edge_at = edge_row[None]
    leftmost, rightmost, edge = column_call(
        edge_kernel, [edge_at], [input_keys, input_values], [16, 16, 32], hbm=True
    )
    core_slots = [
        (permute(input_keys, route), permute(input_values, route)) for route in to_frame
    ]
    leftmost, rightmost = after((leftmost, rightmost), core_slots)
    right = permute(leftmost, to_left)
    left = permute(rightmost, to_right)
    group = lax.axis_index("groups")
    turns = devices // 4
    share = output_matrix.shape[0] // 2
    own = lax.dynamic_slice_in_dim(output_matrix, group * share, share)
    top, low_rows = own[: share // 2], own[share // 2 :]
    bias = window_bias(shifts, frames, jnp.stack([band_idx, col_idx, frame_idx]))
    down = adapter_down_weight.T
    grad_low = (ADAPTER * nt(adapter_up_weight, upstream)).astype(BF16)
    extra = tn(down, grad_low)
    across = swap(after(upstream, bias), 1, 0)
    start = [left, right, own, low_rows, bias, grad_low, extra, combo, across, core_slots]
    if turns == 4:
        one, two = swap(own, 0, 4), swap(top, 0, 8)
        start += [one, two]
    to_outer = column_call(outer_kernel, [edge_at], [after(left, start), right, edge], [40])

    outer = permute(to_outer, to_band)
    beside = swap(after(upstream, to_outer), 0, 2)
    upper = swap(after(across[: TILE // 2], to_outer), 0, 2)
    opened = (outer, beside, upper)
    if turns == 4:
        two_low = swap(after(low_rows, to_outer), 0, 8)
        three = swap(after(two, to_outer), 0, 4)
        opened = (*opened, two_low, three)
        three_low = swap(after(two_low, opened), 0, 4)
        weights = [own, one, two, two_low, three, three_low]
        fetched = [three_low]
    else:
        found = {0: own}
        for bit in [1 << b for b in reversed(range(turns.bit_length() - 1))]:
            found |= {t ^ bit: swap(block, 0, 4 * bit) for t, block in found.items()}
        weights = [found[t] for t in range(turns)]
        fetched = []
    lower = swap(after(beside[TILE // 2 :], opened), 1, 0)
    across_other = swap(after(across, opened), 0, 1)
    fetched.append(lower)

    rim = column_call(rim_kernel, [], [after(left, opened), right, outer], [2 * RIM])
    slots = [(input_keys, input_values, rim)] + [
        (*core, permute(rim, route)) for core, route in zip(core_slots, to_frame)
    ]
    forward = attend(
        combo,
        after(input_queries, extra, across_other),
        slots,
        bias, down, grad_low, upstream,
        turns,
    )
    att, log_total, grads, low, *att_members = after(forward, fetched)

    att_like, att_other = att_members or spread(att, me, turns)
    got = permute(grads[1], [(i, i ^ 1) for i in everyone])
    part = grads[0].astype(F32) + got.astype(F32)

    def add_over(part, bit, until):
        part = part.astype(BF16)
        got = after(permute(part, [(i, i ^ bit) for i in everyone]), until)
        return part.astype(F32) + got.astype(F32), got

    bits = [1 << b for b in range(1, devices.bit_length() - 1)]
    if share % 16:
        weights = [jnp.concatenate(weights)]
    att_packed = pack(att_like, swap(att_other, 0, 1))
    att_got = [swap(pair, x, 2 * y) for (x, y), pair in zip(PLACES[1:], att_packed[1:])]
    upstream_here, across, across_other, beside = in_hbm([upstream, across, across_other, beside])
    tokens = [
        [upstream_here, swap(after(upstream, att), 0, 1)],
        [across, across_other],
        [beside, swap(after(beside, att), 0, 1)],
        [upper, lower, swap(after(upper, att), 0, 1), swap(after(lower, att), 0, 1)],
    ]
    grads_like, grads_other = grad_parts([after(weights[0], att), *weights[1:]], tokens)
    att_of = [att_packed[0], *after(att_got, grads_like)]
    for bit in bits[1:-1]:
        part, got = add_over(part, bit, grads_like)
    grads_packed = pack(grads_like, swap(after(grads_other, att_of), 0, 1))
    grads_got = [swap(pair, x, 2 * y) for (x, y), pair in zip(PLACES[1:], grads_packed[1:])]
    near, sent = [], []
    for half in range(2):
        far = swap(after(project(weights, att_of, 1, half), grads_packed, got), 0, 1)
        keep, send = project(weights, att_of, 0, half, (far,))
        near.append(keep)
        sent.append(swap(send, 1, 0) if half else swap(send, 0, 2))
    grads_of = [grads_packed[0], *after(grads_got, near)]
    part, got = add_over(after(part, grads_of), bits[-1], near)
    grad_att = collect(grads_of, me, turns)
    grad_query, terms = attend_back(
        combo, after(input_queries, near), slots, bias, att, grad_att, extra, log_total
    )
    grad_query, terms = after((grad_query, terms), sent, got)
    core, rim_terms = terms[0]
    rim_terms = rim_terms.astype(F32)
    back = [[(j, i) for i, j in route] for route in to_frame]
    for (_, block), route in zip(terms[1:], back):
        rim_terms += permute(block, route).astype(F32)
    core_terms = [core] + [
        permute(after(block, rim_terms), route) for (block, _), route in zip(terms[1:], back)
    ]
    keys_out, values_out = rim_terms[:RIM], rim_terms[RIM:]
    to_outer = jnp.concatenate(
        [keys_out[16:32], values_out[16:32], keys_out[32:34], values_out[32:34]]
    ).astype(BF16)
    outer = permute(to_outer, to_band)
    sent = after(sent, to_outer)
    first, second_half = (
        keep.astype(F32) + block.astype(F32) for keep, block in zip(near, sent)
    )
    part, _ = add_over(part, bits[0], outer)
    last_rows = swap(first[1].astype(BF16), 1, 0), swap(second_half[1].astype(BF16), 0, 2)
    at_edge = (jnp.arange(ROWS)[:, None] == edge_row).astype(F32)
    outer_corners = outer[32:].astype(F32)

    def side(number):
        at = 8 * number
        return jnp.concatenate(
            [
                keys_out[at : at + 8] + at_edge * outer_corners[number],
                values_out[at : at + 8] + at_edge * outer_corners[2 + number],
            ]
        ).astype(BF16)

    sides = side(0), side(1)
    from_right = permute(sides[0], to_left)
    from_left = permute(sides[1], to_right)
    last_rows = after(last_rows, sides)
    first = first[0] + last_rows[0].astype(F32)
    second_half = second_half[0] + last_rows[1].astype(F32)
    projected = (
        jnp.concatenate([first, second_half], axis=1) + ADAPTER * tn(low, adapter_up_weight)
    ).astype(BF16)

    part = after(part.astype(BF16), last_rows)
    other = after(permute(part, [(i, i ^ 1) for i in everyone]), sides)
    grad_down = jnp.where(second == 0, part, other).astype(F32).T
    grad_up = jnp.where(second == 0, other, part).astype(F32)

    from_left, from_right = after((from_left, from_right), projected, grad_down, grad_up)
    cell = jnp.arange(TILE, dtype=jnp.int32)
    mark = jnp.arange(32, dtype=jnp.int32)
    source = jnp.where(
        mark < 8,
        mark * TCOLS,
        jnp.where(mark < 16, (mark - 8) * TCOLS + TCOLS - 1, edge_row * TCOLS + mark - 16),
    )
    pick = (source[:, None] == cell[None, :]).astype(BF16)
    gathered = [
        jnp.concatenate([from_left[at : at + 8], from_right[at : at + 8], outer[row : row + 16]])
        for at, row in ((0, 0), (8, 16))
    ]
    grad_key, grad_value = (
        (
            sum(block[rows].astype(F32) for block in core_terms) + tn(pick, got)
        ).astype(BF16)
        for rows, got in ((slice(0, TILE), gathered[0]), (slice(TILE, None), gathered[1]))
    )
    return (projected, grad_query, grad_key, grad_value, grad_down, grad_up)


def solution(mesh):
    tokens = P(("groups", "tensor"), None)
    return jax.shard_map(
        on_device,
        mesh=mesh,
        in_specs=(tokens, tokens, tokens, P("tensor", None), P(), P(), tokens, P(), P()),
        out_specs=(tokens, tokens, tokens, tokens, P("groups", None), P("groups", None)),
        check_vma=False,
    )
```

```python
import functools

import jax
import jax.numpy as jnp
from jax import lax
from jax.experimental import pallas as pl
from jax.experimental.pallas import tpu as pltpu
from jax.sharding import PartitionSpec as P

ROWS = 8
CTILES = 4
BANDS = 2
TCOLS = 16
TILE = ROWS * TCOLS
RIM = 48
SLOT = TILE + RIM
HEAD = 128
STEP = 8

SCALE = HEAD**-0.5
ADAPTER = 0.5
F32 = jnp.float32
BF16 = jnp.bfloat16


def nn(a, b):
    return jnp.dot(a, b, preferred_element_type=F32)


def nt(a, b):
    return lax.dot_general(a, b, (((1,), (1,)), ((), ())), preferred_element_type=F32)


def tn(a, b):
    return lax.dot_general(a, b, (((0,), (0,)), ((), ())), preferred_element_type=F32)


def slot_keys(slots, cols):
    keys, values = [], []
    for core_keys, core_values, rim in slots:
        keys += [core_keys[:, cols], rim[:RIM, cols]]
        values += [core_values[:, cols], rim[RIM:, cols]]
    return jnp.concatenate(keys, axis=0), jnp.concatenate(values, axis=0)


def forward_kernel(n_slots, turns, combo, query, *refs):
    slots = [refs[3 * i : 3 * i + 3] for i in range(n_slots)]
    bias, down, grad_low, upstream, att_ref, log_ref, grads_ref, low_ref = refs[
        3 * n_slots : 3 * n_slots + 8
    ]
    low_acc, members = refs[-1], refs[3 * n_slots + 8 : -1]
    step = pl.program_id(0)
    second = combo.shape[0] - 2

    @pl.when(step == 0)
    def _():
        low_acc[...] = jnp.zeros_like(low_acc)

    columns = [slice(i * HEAD, (i + 1) * HEAD) for i in range(STEP)]
    pairs = [slot_keys(slots, cols) for cols in columns]
    scores = [
        nt(keys, query[:, cols]) * SCALE + bias[combo[step * STEP + i]]
        for i, (cols, (keys, _)) in enumerate(zip(columns, pairs))
    ]
    tops = [jnp.max(block, axis=0, keepdims=True) for block in scores]
    weights = [jnp.exp(block - top) for block, top in zip(scores, tops)]
    totals = [jnp.sum(block, axis=0, keepdims=True) for block in weights]
    mixed = [tn(values, block.astype(BF16)) for (_, values), block in zip(pairs, weights)]
    att = jnp.concatenate(
        [(block * (1.0 / total)).astype(BF16) for block, total in zip(mixed, totals)]
    )
    att_ref[...] = att
    if members:
        rows = STEP * HEAD
        members[2][pl.ds(pl.multiple_of(step * rows, rows), rows), :] = att
    log_ref[0] = jnp.concatenate([top + jnp.log(total) for top, total in zip(tops, totals)])
    low_acc[...] += nn(down[...], att)
    at = pl.ds(pl.multiple_of(step * STEP * HEAD, STEP * HEAD), STEP * HEAD)
    grads_ref[combo[second], :, at] = nt(grad_low[...], att).astype(BF16)

    @pl.when(step == pl.num_programs(0) - 1)
    def _():
        low = low_acc[...].astype(BF16)
        low_ref[...] = low
        if members:
            spread_kernel(turns, combo[second + 1], members[2], *members[:2])
        grads_ref[1 - combo[second]] = (ADAPTER * nn(low, upstream[...])).astype(BF16)


def backward_kernel(n_slots, combo, query, *refs):
    slots = [refs[3 * i : 3 * i + 3] for i in range(n_slots)]
    bias, att, grad, extra, log_total, grad_query = refs[3 * n_slots : 3 * n_slots + 6]
    terms = refs[3 * n_slots + 6 :]
    step = pl.program_id(0)
    columns = [slice(i * HEAD, (i + 1) * HEAD) for i in range(STEP)]
    pairs = [slot_keys(slots, cols) for cols in columns]
    scores = [
        nt(keys, query[:, cols]) * SCALE + bias[combo[step * STEP + i]]
        for i, (cols, (keys, _)) in enumerate(zip(columns, pairs))
    ]
    grad_att = [(grad[cols, :].astype(F32) + extra[cols, :]).astype(BF16) for cols in columns]
    grad_probs = [nn(values, block) for (_, values), block in zip(pairs, grad_att)]
    inner = [
        jnp.sum(block.astype(F32) * att[cols, :].astype(F32), axis=0, keepdims=True)
        for block, cols in zip(grad_att, columns)
    ]
    probs = [jnp.exp(block - log_total[0, i : i + 1, :]) for i, block in enumerate(scores)]
    grad_scores = [
        (p * (gp - minus)).astype(BF16) for p, gp, minus in zip(probs, grad_probs, inner)
    ]
    for i, cols in enumerate(columns):
        value_terms = nt(probs[i].astype(BF16), grad_att[i]).astype(BF16)
        key_terms = (nn(grad_scores[i], query[:, cols]) * SCALE).astype(BF16)
        grad_query[:, cols] = (tn(grad_scores[i], pairs[i][0]) * SCALE).astype(BF16)
        for s in range(n_slots):
            core, rim = terms[2 * s : 2 * s + 2]
            at = s * SLOT
            core[:TILE, cols] = key_terms[at : at + TILE]
            core[TILE:, cols] = value_terms[at : at + TILE]
            rim[:RIM, cols] = key_terms[at + TILE : at + SLOT]
            rim[RIM:, cols] = value_terms[at + TILE : at + SLOT]


def column_block(rows):
    return pl.BlockSpec((rows, STEP * HEAD), lambda step, *_: (0, step))


def row_block():
    return pl.BlockSpec((STEP * HEAD, TILE), lambda step, *_: (step, 0))


def whole(shape):
    return pl.BlockSpec(shape, lambda *_: (0,) * len(shape))


def head_call(kernel, n_slots, steps, in_specs, out_specs, out_shape, scratch):
    call = pl.pallas_call(
        kernel,
        grid_spec=pltpu.PrefetchScalarGridSpec(
            num_scalar_prefetch=1,
            grid=(steps,),
            in_specs=in_specs,
            out_specs=out_specs,
            scratch_shapes=scratch,
        ),
        out_shape=out_shape,
        compiler_params=pltpu.CompilerParams(
            dimension_semantics=("arbitrary",), vmem_limit_bytes=max(2, n_slots) * 7 * 1024 * 1024
        ),
        cost_estimate=pl.CostEstimate(flops=1000, bytes_accessed=1000, transcendentals=0),
    )

    def from_hbm(scalars, *arrays):
        return call(scalars, *in_hbm(arrays[:3]), *arrays[3:])

    return from_hbm


def in_hbm(arrays):
    return [pltpu.with_memory_space_constraint(array, pltpu.HBM) for array in arrays]


def slot_specs(n_slots):
    return [column_block(TILE), column_block(TILE), column_block(2 * RIM)] * n_slots


def attend(combo, query, slots, bias, down, grad_low, upstream, turns):
    tokens, width = query.shape
    heads = width // HEAD
    rank = down.shape[0]
    n_slots = len(slots)
    aligned = width // (8 * turns) % 16 == 0
    member = (4, width // 8, tokens)
    return head_call(
        functools.partial(forward_kernel, n_slots, turns),
        n_slots,
        heads // STEP,
        [column_block(tokens)]
        + slot_specs(n_slots)
        + [
            whole(bias.shape),
            column_block(rank),
            whole(grad_low.shape),
            whole(upstream.shape),
        ],
        [
            row_block(),
            pl.BlockSpec((1, STEP, tokens), lambda step, *_: (step, 0, 0)),
            whole((2, rank, width)),
            whole((rank, tokens)),
        ]
        + [whole(member)] * 2 * aligned,
        [
            pltpu.HBM((width, tokens), BF16),
            jax.ShapeDtypeStruct((heads // STEP, STEP, tokens), F32),
            jax.ShapeDtypeStruct((2, rank, width), BF16),
            jax.ShapeDtypeStruct((rank, tokens), BF16),
        ]
        + [jax.ShapeDtypeStruct(member, BF16)] * 2 * aligned,
        [pltpu.VMEM((width, tokens), BF16)] * aligned + [pltpu.VMEM((rank, tokens), F32)],
    )(
        combo, query, *[part for slot in slots for part in slot], bias, *in_hbm([down]), grad_low,
        *in_hbm([upstream]),
    )


def attend_back(combo, query, slots, bias, att, grad, extra, log_total):
    tokens, width = query.shape
    heads = width // HEAD
    n_slots = len(slots)
    out = head_call(
        functools.partial(backward_kernel, n_slots),
        n_slots,
        heads // STEP,
        [column_block(tokens)]
        + slot_specs(n_slots)
        + [
            whole(bias.shape),
            row_block(),
            row_block(),
            row_block(),
            pl.BlockSpec((1, STEP, tokens), lambda step, *_: (step, 0, 0)),
        ],
        [column_block(tokens)] + [column_block(2 * TILE), column_block(2 * RIM)] * n_slots,
        [pltpu.HBM((tokens, width), BF16)]
        + [pltpu.HBM((2 * TILE, width), BF16), pltpu.HBM((2 * RIM, width), BF16)] * n_slots,
        [],
    )(
        combo, query, *[part for slot in slots for part in slot], bias, *in_hbm([att]), grad, extra,
        log_total,
    )
    return out[0], [out[1 + 2 * s : 3 + 2 * s] for s in range(n_slots)]


PLACES = [(x, y) for y in range(2) for x in range(2)]
MEMBERS = [(x, y, c) for x, y in PLACES for c in range(2)]


def block_of(member, turn):
    x, y, c = member
    return turn * 8 + y * 4 + c * 2 + x


def plain_call(kernel, grid, in_specs, out_specs, out_shape, scratch):
    return pl.pallas_call(
        kernel,
        grid=grid,
        in_specs=in_specs,
        out_specs=out_specs,
        out_shape=out_shape,
        scratch_shapes=scratch,
        compiler_params=pltpu.CompilerParams(
            dimension_semantics=("arbitrary",) * len(grid), vmem_limit_bytes=14 * 1024 * 1024
        ),
        cost_estimate=pl.CostEstimate(flops=1000, bytes_accessed=1000, transcendentals=0),
    )


def spread_kernel(turns, me, rows_ref, *outs):
    size = rows_ref.shape[0] // (8 * turns)
    for number, member in enumerate(MEMBERS):
        for turn in range(turns):
            at = pl.multiple_of((block_of(member, turn) ^ me) * size, size)
            outs[number % 2][number // 2, turn * size : (turn + 1) * size, :] = rows_ref[
                pl.ds(at, size), :
            ]


def collect_kernel(turns, me, *refs):
    out = refs[-1]
    size = out.shape[0] // (8 * turns)
    for number, member in enumerate(MEMBERS):
        part = refs[number // 2].at[number % 2]
        for turn in range(turns):
            at = pl.multiple_of((block_of(member, turn) ^ me[0]) * size, size)
            out[pl.ds(at, size), :] = part[turn * size : (turn + 1) * size, :]


SCALARS = pl.BlockSpec(memory_space=pltpu.SMEM)


def spread(rows, me, turns):
    total, tokens = rows.shape
    size = total // (8 * turns)
    blocks = rows.reshape(8 * turns, size, tokens)
    order = [[block_of((x, y, c), t) for x, y in PLACES for t in range(turns)] for c in range(2)]
    return [
        jnp.take(blocks, me ^ jnp.array(o), axis=0).reshape(4, turns * size, tokens) for o in order
    ]


def collect(parts, me, turns):
    _, rows, tokens = parts[0].shape
    size = rows // turns
    total = 8 * rows
    if size % 16:
        every = [parts[number // 2][number % 2] for number in range(8)]
        blocks = jnp.concatenate(every).reshape(8 * turns, size, tokens)
        slot = {block_of(m, t): i * turns + t for i, m in enumerate(MEMBERS) for t in range(turns)}
        order = jnp.array([slot[b] for b in range(8 * turns)])
        return jnp.take(blocks, order[me ^ jnp.arange(8 * turns)], axis=0).reshape(total, tokens)
    return plain_call(
        functools.partial(collect_kernel, turns),
        (1,),
        [SCALARS] + [whole(part.shape) for part in parts],
        whole((total, tokens)),
        jax.ShapeDtypeStruct((total, tokens), parts[0].dtype),
        [],
    )(me[None], *in_hbm(parts[:1]), *parts[1:])


def edge_kernel(where, keys, values, to_left, to_right, edge):
    mark = lax.broadcasted_iota(jnp.int32, (32, TILE), 0)
    cell = lax.broadcasted_iota(jnp.int32, (32, TILE), 1)
    side = jnp.where(mark < 8, mark * TCOLS, (mark - 8) * TCOLS + TCOLS - 1)
    source = jnp.where(mark < 16, side, where[0] * TCOLS + mark - 16)
    pick = (source == cell).astype(F32).astype(BF16)
    key_edges = nn(pick, keys[...])
    value_edges = nn(pick, values[...])
    to_left[...] = jnp.concatenate([key_edges[:8], value_edges[:8]]).astype(BF16)
    to_right[...] = jnp.concatenate([key_edges[8:16], value_edges[8:16]]).astype(BF16)
    edge[...] = jnp.concatenate([key_edges[16:], value_edges[16:]]).astype(BF16)


def outer_kernel(where, left, right, edge, outer):
    sides = [left[...].astype(F32), right[...].astype(F32)]
    last = where[0] == ROWS - 1
    corners = [
        jnp.where(last, side[at + ROWS - 1 : at + ROWS], side[at : at + 1])
        for at in (0, 8)
        for side in sides
    ]
    blank = jnp.zeros((4, edge.shape[1]), F32)
    outer[...] = jnp.concatenate([edge[...].astype(F32), *corners, blank]).astype(BF16)


def rim_kernel(left, right, outer, rim):
    sides = [left[...].astype(F32), right[...].astype(F32)]
    far = outer[...].astype(F32)
    blank = jnp.zeros((14, far.shape[1]), F32)
    rim[...] = jnp.concatenate(
        [
            sides[0][:8], sides[1][:8], far[:16], far[32:34], blank,
            sides[0][8:], sides[1][8:], far[16:32], far[34:36], blank,
        ]
    ).astype(BF16)


def column_call(kernel, scalars, blocks, out_rows, hbm=False):
    width = blocks[0].shape[1]
    step = width // 4
    out = plain_call(
        kernel,
        (4,),
        [SCALARS] * len(scalars)
        + [pl.BlockSpec((block.shape[0], step), lambda j: (0, j)) for block in blocks],
        [pl.BlockSpec((rows, step), lambda j: (0, j)) for rows in out_rows],
        [(pltpu.HBM if hbm else jax.ShapeDtypeStruct)((rows, width), BF16) for rows in out_rows],
        [],
    )(*scalars, *(in_hbm(blocks) if hbm else blocks))
    return out if len(out_rows) > 1 else out[0]


def pack_kernel(here, there, *outs):
    for place, out in enumerate(outs):
        out[0] = here[place]
        out[1] = there[place]


def pack(here, there):
    _, rows, tokens = here.shape
    return plain_call(
        pack_kernel,
        (1,),
        [whole(here.shape)] * 2,
        [whole((2, rows, tokens))] * 4,
        [pltpu.HBM((2, rows, tokens), BF16)]
        + [jax.ShapeDtypeStruct((2, rows, tokens), BF16)] * 3,
        [],
    )(here, there)


def weight_block(refs):
    return jnp.concatenate([ref[...] for ref in refs], axis=0) if len(refs) > 1 else refs[0][...]


def grad_kernel(n_parts, counts, *refs):
    weights, tokens, outs, acc = refs[:n_parts], refs[n_parts:-3], refs[-3:-1], refs[-1]
    step = pl.program_id(0)

    @pl.when(step == 0)
    def _():
        acc[...] = jnp.zeros_like(acc)

    weight = weight_block(weights)
    at = 0
    for place, count in enumerate(counts):
        here = jnp.concatenate([ref[...] for ref in tokens[at : at + count]], axis=0)
        acc[place] += nt(weight, here)
        at += count

    @pl.when(step == pl.num_programs(0) - 1)
    def _():
        for place in range(4):
            outs[0][place] = acc[place, :, :TILE].astype(BF16)
            outs[1][place] = acc[place, :, TILE:].astype(BF16)


def grad_parts(weights, tokens):
    rows = sum(part.shape[0] for part in weights)
    width = weights[0].shape[1]
    step = 1536
    counts = [len(parts) for parts in tokens]
    tokens = [part for parts in tokens for part in parts]
    return plain_call(
        functools.partial(grad_kernel, len(weights), counts),
        (width // step,),
        [pl.BlockSpec((part.shape[0], step), lambda k: (0, k)) for part in (*weights, *tokens)],
        [whole((4, rows, TILE))] * 2,
        [jax.ShapeDtypeStruct((4, rows, TILE), BF16)] * 2,
        [pltpu.VMEM((4, rows, 2 * TILE), F32)],
    )(*in_hbm(weights), *tokens)


def project_kernel(n_parts, core, kept, *refs):
    weights, parts, rest = refs[:n_parts], refs[n_parts : n_parts + 4], refs[n_parts + 4 :]
    turned = rest[-1]

    @pl.when(pl.program_id(0) == 0)
    def _():
        for place in range(4):
            turned[place * TILE : (place + 1) * TILE, :] = parts[place][core].T

    result = nn(turned[...], weight_block(weights))
    blocks = [result[place * TILE : (place + 1) * TILE] for place in range(4)]
    if core:
        for place in range(4):
            rest[0][place] = blocks[place].astype(BF16)
    else:
        added, keep, send = rest[:-1]
        for out, places in ((keep, kept), (send, [p for p in range(4) if p not in kept])):
            for slot, place in enumerate(places):
                out[slot] = (blocks[place] + added[place].astype(F32)).astype(BF16)


def project(weights, parts, core, half, added=()):
    rows = sum(part.shape[0] for part in weights)
    width = weights[0].shape[1] // 2
    step = 768
    split = width // step
    kept = [0, 2] if half else [0, 1]
    four = pl.BlockSpec((4, TILE, step), lambda j: (0, 0, j))
    two = pl.BlockSpec((2, TILE, step), lambda j: (0, 0, j))
    shape = (2, TILE, width)
    return plain_call(
        functools.partial(project_kernel, len(weights), core, kept),
        (split,),
        [pl.BlockSpec((part.shape[0], step), lambda j: (0, half * split + j)) for part in weights]
        + [whole(part.shape) for part in parts]
        + [four] * len(added),
        four if core else [two] * 2,
        jax.ShapeDtypeStruct((4, TILE, width), BF16)
        if core
        else [pltpu.HBM(shape, BF16), jax.ShapeDtypeStruct(shape, BF16)],
        [pltpu.VMEM((4 * TILE, rows), BF16)],
    )(*in_hbm(weights), *in_hbm(parts[:1]), *parts[1:], *added)


def bias_kernel(shifts, frames, where, bias):
    band_idx, col_idx, frame_idx = where[0], where[1], where[2]
    at = lax.broadcasted_iota(jnp.int32, (SLOT, TILE), 0)
    query = lax.broadcasted_iota(jnp.int32, (SLOT, TILE), 1)
    rim = at - TILE
    outer = jnp.where(band_idx == 0, ROWS, -1)
    row = jnp.where(rim < 0, at // TCOLS, jnp.where(rim < 16, rim % ROWS, outer))
    col = jnp.where(rim < 16, jnp.where(rim < 8, -1, TCOLS), rim - 16)
    col = jnp.where(rim < 0, at % TCOLS, jnp.where(rim < 32, col, (rim - 32) * (TCOLS + 1) - 1))
    across = col_idx * TCOLS + col
    near = (jnp.abs(col - query % TCOLS) <= 1) & (rim < 34)
    near &= (across >= 0) & (across < CTILES * TCOLS)
    gap = jnp.abs(row - query // TCOLS)
    for row_reach in range(2):
        space = jnp.where(near & (gap <= row_reach), 0.0, -1e30)
        for slot, shift in enumerate(shifts):
            there = (frame_idx + shift >= 0) & (frame_idx + shift < frames) | (frames == 2)
            for frame_reach in range(2):
                time = jnp.where(there & (abs(shift) <= frame_reach), 0.0, -1e30)
                bias[2 * frame_reach + row_reach, slot * SLOT : (slot + 1) * SLOT, :] = (
                    jnp.minimum(space, time)
                )


def window_bias(shifts, frames, where):
    shape = (4, len(shifts) * SLOT, TILE)
    return plain_call(
        functools.partial(bias_kernel, shifts, frames),
        (1,),
        [SCALARS],
        whole(shape),
        jax.ShapeDtypeStruct(shape, F32),
        [],
    )(where)


def permute(block, route):
    return lax.ppermute(block, "tensor", route)


def swap(block, group_bit, bits):
    groups, devices = lax.axis_size("groups"), lax.axis_size("tensor")
    return lax.ppermute(
        block,
        ("groups", "tensor"),
        [
            (g * devices + i, (g ^ group_bit) * devices + (i ^ bits))
            for g in range(groups)
            for i in range(devices)
        ],
    )


def after(value, *done):
    return lax.optimization_barrier((value, done))[0]


def on_device(
    input_queries,
    input_keys,
    input_values,
    output_matrix,
    adapter_down_weight,
    adapter_up_weight,
    upstream,
    window_frame_reach,
    window_row_reach,
):
    devices = lax.axis_size("tensor")
    frames = devices // (BANDS * CTILES)
    position = lax.axis_index("tensor")
    frame_idx = position % frames
    col_idx = position // frames % CTILES
    band_idx = position // (frames * CTILES)
    everyone = range(devices)
    to_right = [(i, i + frames) for i in everyone if i // frames % CTILES < CTILES - 1]
    to_left = [(j, i) for i, j in to_right]
    to_band = [(i, (i + devices // BANDS) % devices) for i in everyone]
    if frames == 1:
        shifts, to_frame = [0], []
    elif frames == 2:
        shifts, to_frame = [0, 1], [[(i, i ^ 1) for i in everyone]]
    else:
        later = [(i, i + 1) for i in everyone if i % frames < frames - 1]
        shifts, to_frame = [0, -1, 1], [later, [(j, i) for i, j in later]]
    edge_row = jnp.where(band_idx == 0, ROWS - 1, 0)
    second = position % 2
    me = position * 2 + lax.axis_index("groups")
    combo = jnp.append(2 * window_frame_reach + window_row_reach, jnp.stack([second, me]))

    edge_at = edge_row[None]
    leftmost, rightmost, edge = column_call(
        edge_kernel, [edge_at], [input_keys, input_values], [16, 16, 32], hbm=True
    )
    core_slots = [
        (permute(input_keys, route), permute(input_values, route)) for route in to_frame
    ]
    leftmost, rightmost = after((leftmost, rightmost), core_slots)
    right = permute(leftmost, to_left)
    left = permute(rightmost, to_right)
    group = lax.axis_index("groups")
    turns = devices // 4
    share = output_matrix.shape[0] // 2
    own = lax.dynamic_slice_in_dim(output_matrix, group * share, share)
    top, low_rows = own[: share // 2], own[share // 2 :]
    bias = window_bias(shifts, frames, jnp.stack([band_idx, col_idx, frame_idx]))
    down = adapter_down_weight.T
    grad_low = (ADAPTER * nt(adapter_up_weight, upstream)).astype(BF16)
    extra = tn(down, grad_low)
    across = swap(after(upstream, bias), 1, 0)
    start = [left, right, own, low_rows, bias, grad_low, extra, combo, across, core_slots]
    if turns == 4:
        one, two = swap(own, 0, 4), swap(top, 0, 8)
        start += [one, two]
    to_outer = column_call(outer_kernel, [edge_at], [after(left, start), right, edge], [40])

    outer = permute(to_outer, to_band)
    beside = swap(after(upstream, to_outer), 0, 2)
    upper = swap(after(across[: TILE * 5 // 8], to_outer), 0, 2)
    opened = (outer, beside, upper)
    if turns == 4:
        two_low = swap(after(low_rows, to_outer), 0, 8)
        three = swap(after(two, to_outer), 0, 4)
        opened = (*opened, two_low, three)
        three_low = swap(after(two_low, opened), 0, 4)
        weights = [own, one, two, two_low, three, three_low]
        fetched = [three_low]
    else:
        found = {0: own}
        for bit in [1 << b for b in reversed(range(turns.bit_length() - 1))]:
            found |= {t ^ bit: swap(block, 0, 4 * bit) for t, block in found.items()}
        weights = [found[t] for t in range(turns)]
        fetched = []
    lower = swap(after(beside[TILE * 5 // 8 :], opened), 1, 0)
    across_other = swap(after(across, opened), 0, 1)
    beside_other = swap(after(beside, opened), 0, 1)
    fetched += [lower, beside_other]

    rim = column_call(rim_kernel, [], [after(left, opened), right, outer], [2 * RIM])
    slots = [(input_keys, input_values, rim)] + [
        (*core, permute(rim, route)) for core, route in zip(core_slots, to_frame)
    ]
    forward = attend(
        combo,
        after(input_queries, extra, across_other),
        slots,
        bias, down, grad_low, upstream,
        turns,
    )
    att, log_total, grads, low, *att_members = after(forward, fetched)

    att_like, att_other = att_members or spread(att, me, turns)
    got = permute(grads[1], [(i, i ^ 1) for i in everyone])
    part = grads[0].astype(F32) + got.astype(F32)

    def add_over(part, bit, until):
        part = part.astype(BF16)
        got = after(permute(part, [(i, i ^ bit) for i in everyone]), until)
        return part.astype(F32) + got.astype(F32), got

    bits = [1 << b for b in range(1, devices.bit_length() - 1)]
    if share % 16:
        weights = [jnp.concatenate(weights)]
    att_packed = pack(att_like, swap(att_other, 0, 1))
    att_got = [swap(pair, x, 2 * y) for (x, y), pair in zip(PLACES[1:], att_packed[1:])]
    upstream_here, across, across_other, beside = in_hbm([upstream, across, across_other, beside])
    tokens = [
        [upstream_here, swap(after(upstream, att_packed), 0, 1)],
        [across, across_other],
        [beside, beside_other],
        [upper, lower, swap(after(upper, att_packed), 0, 1), swap(after(lower, att), 0, 1)],
    ]
    grads_like, grads_other = grad_parts([after(weights[0], att, got), *weights[1:]], tokens)
    att_of = [att_packed[0], *after(att_got, grads_like)]
    for bit in bits[1:-1]:
        part, got = add_over(part, bit, grads_like)
    grads_packed = pack(grads_like, swap(after(grads_other, att_of), 0, 1))
    grads_got = [swap(pair, x, 2 * y) for (x, y), pair in zip(PLACES[1:], grads_packed[1:])]
    near, sent = [], []
    for half in range(2):
        far = swap(after(project(weights, att_of, 1, half), grads_packed, got), 0, 1)
        keep, send = project(weights, att_of, 0, half, (far,))
        near.append(keep)
        sent.append(swap(send, 1, 0) if half else swap(send, 0, 2))
    grads_of = [grads_packed[0], *after(grads_got, near)]
    part, got = add_over(after(part, grads_of), bits[-1], near)
    grad_att = collect(grads_of, me, turns)
    grad_query, terms = attend_back(
        combo, after(input_queries, near), slots, bias, att, grad_att, extra, log_total
    )
    grad_query, terms = after((grad_query, terms), sent, got)
    core, rim_terms = terms[0]
    rim_terms = rim_terms.astype(F32)
    back = [[(j, i) for i, j in route] for route in to_frame]
    for (_, block), route in zip(terms[1:], back):
        rim_terms += permute(block, route).astype(F32)
    core_terms = [core] + [
        permute(after(block, rim_terms), route) for (block, _), route in zip(terms[1:], back)
    ]
    keys_out, values_out = rim_terms[:RIM], rim_terms[RIM:]
    to_outer = jnp.concatenate(
        [keys_out[16:32], values_out[16:32], keys_out[32:34], values_out[32:34]]
    ).astype(BF16)
    outer = permute(to_outer, to_band)
    sent = after(sent, to_outer)
    first, second_half = (
        keep.astype(F32) + block.astype(F32) for keep, block in zip(near, sent)
    )
    part, _ = add_over(part, bits[0], outer)
    last_rows = swap(first[1].astype(BF16), 1, 0), swap(second_half[1].astype(BF16), 0, 2)
    at_edge = (jnp.arange(ROWS)[:, None] == edge_row).astype(F32)
    outer_corners = outer[32:].astype(F32)

    def side(number):
        at = 8 * number
        return jnp.concatenate(
            [
                keys_out[at : at + 8] + at_edge * outer_corners[number],
                values_out[at : at + 8] + at_edge * outer_corners[2 + number],
            ]
        ).astype(BF16)

    sides = side(0), side(1)
    from_right = permute(sides[0], to_left)
    from_left = permute(sides[1], to_right)
    last_rows = after(last_rows, sides)
    first = first[0] + last_rows[0].astype(F32)
    second_half = second_half[0] + last_rows[1].astype(F32)
    projected = (
        jnp.concatenate([first, second_half], axis=1) + ADAPTER * tn(low, adapter_up_weight)
    ).astype(BF16)

    part = after(part.astype(BF16), last_rows)
    other = after(permute(part, [(i, i ^ 1) for i in everyone]), sides)
    grad_down = jnp.where(second == 0, part, other).astype(F32).T
    grad_up = jnp.where(second == 0, other, part).astype(F32)

    from_left, from_right = after((from_left, from_right), projected, grad_down, grad_up)
    cell = jnp.arange(TILE, dtype=jnp.int32)
    mark = jnp.arange(32, dtype=jnp.int32)
    source = jnp.where(
        mark < 8,
        mark * TCOLS,
        jnp.where(mark < 16, (mark - 8) * TCOLS + TCOLS - 1, edge_row * TCOLS + mark - 16),
    )
    pick = (source[:, None] == cell[None, :]).astype(BF16)
    gathered = [
        jnp.concatenate([from_left[at : at + 8], from_right[at : at + 8], outer[row : row + 16]])
        for at, row in ((0, 0), (8, 16))
    ]
    grad_key, grad_value = (
        (
            sum(block[rows].astype(F32) for block in core_terms) + tn(pick, got)
        ).astype(BF16)
        for rows, got in ((slice(0, TILE), gathered[0]), (slice(TILE, None), gathered[1]))
    )
    return (projected, grad_query, grad_key, grad_value, grad_down, grad_up)


def solution(mesh):
    tokens = P(("groups", "tensor"), None)
    return jax.shard_map(
        on_device,
        mesh=mesh,
        in_specs=(tokens, tokens, tokens, P("tensor", None), P(), P(), tokens, P(), P()),
        out_specs=(tokens, tokens, tokens, tokens, P("groups", None), P("groups", None)),
        check_vma=False,
    )
```
